512 devices in a mesh: blk: 32 (over y_lo, z), gather: 16 (over y_hi, x, core).
Axes of the slice: x: 4, y: 4 (y_hi: 2, y_lo: 2; y = y_hi * 2 + y_lo), z: 16, core: 2. Of those that a mesh axis runs over, the one named last changes fastest.
Arguments:
- images: bfloat16 [65536, 1152], P(('blk', 'gather')), may hold values from -0.1796875 to 0.1796875
- captions: bfloat16 [65536, 1152], P(('blk', 'gather')), may hold values from -0.1796875 to 0.1796875
- pair_index: int32 [32, 2048], P('blk', 'gather'), may hold values from 0 to 2047, each once within a row
- logit_scale: float32 [1], replicated, may hold values from 1.5 to 2.5
- logit_bias: float32 [1], replicated, may hold values from -4 to -1
Outputs:
- loss_mean: float32 [1], replicated
- grad_images: float32 [65536, 1152], P(('blk', 'gather'))
- grad_captions: float32 [65536, 1152], P(('blk', 'gather'))
- grad_scale: float32 [1], replicated
- grad_bias: float32 [1], replicated
The draws below stay inside these ranges and needn't reach their ends.
Inputs may be any that keep to these rules, and one draw needn't show every extreme that they name: Each row of pair_index is a permutation of 0 to 2047.
All inputs are finite; a program needn't handle non-finite values.
Results may differ from the reference program's by a relative error of at most 0.00075.
Values may be sent and summed in bfloat16 or wider, within the bound.
A program may use at most 64 MiB of HBM per device.

```python
import jax
import jax.numpy as jnp
from jax import lax

E = 1152
WINDOW = 2
BLOCK = 2048
TOTAL = 65536
N_BLK = 32


LIMIT = 0.1796875


def common_parts(key):
    direction = jax.random.normal(jax.random.fold_in(key, 101), (E,), jnp.float32)
    order = jax.random.permutation(jax.random.fold_in(key, 102), N_BLK)
    strength = 1.2 * order.astype(jnp.float32) / (N_BLK - 1)
    return (direction, strength)


def assemble(noise, row_factor, row_scale, direction, strength):
    block_strength = jnp.repeat(strength, BLOCK, total_repeat_length=TOTAL)[:, None]
    rows = 0.03 * row_scale * (noise + block_strength * row_factor * direction[None, :])
    return jnp.clip(rows, -LIMIT, LIMIT).astype(jnp.bfloat16)


def draw_images(key, part):
    direction, strength = common_parts(key)
    key = jax.random.fold_in(key, 1)
    first, second = jax.random.split(key, 2)
    noise = jax.random.normal(first, (TOTAL, E), jnp.float32)
    row_factor = jax.random.uniform(second, (TOTAL, 1), jnp.float32, 0.3, 1.7)
    row_scale = jnp.ones((TOTAL, 1), jnp.float32)
    return assemble(noise, row_factor, row_scale, direction, strength)


def draw_captions(key, part):
    direction, strength = common_parts(key)
    key = jax.random.fold_in(key, 2)
    first, second = jax.random.split(key, 2)
    noise = jax.random.normal(first, (TOTAL, E), jnp.float32)
    row_factor = jax.random.uniform(second, (TOTAL, 1), jnp.float32, 0.3, 1.7)
    row_scale = jnp.ones((TOTAL, 1), jnp.float32)
    return assemble(noise, row_factor, row_scale, direction, strength)


def setup_inputs(seed: int = 0) -> dict:
    seeds = jax.random.split(jax.random.key(seed), 6)
    return {
        "images": draw_images(jax.random.fold_in(seeds[5], 71), 0),
        "captions": draw_captions(jax.random.fold_in(seeds[5], 71), 0),
        "pair_index": jax.vmap(lambda own: jax.random.permutation(own, BLOCK))(jax.random.split(seeds[2], N_BLK)).reshape((N_BLK, BLOCK)).astype(jnp.int32),
        "logit_scale": jnp.clip(jax.random.uniform(seeds[3], (1,), jnp.float32, 1.5, 2.5), 1.5, 2.5),
        "logit_bias": jnp.clip(jax.random.uniform(seeds[4], (1,), jnp.float32, -4.0, -1.0), -4.0, -1.0),
    }


EPS = 1e-06

def normalize(embedded):
    widened = embedded.astype(jnp.float32)
    inverse = lax.rsqrt(lax.optimization_barrier(jnp.sum(widened * widened, axis=-1, keepdims=True)) + EPS)
    return (widened * inverse, inverse)

def backnorm(unit, inverse, upstream):
    return inverse * (upstream - unit * lax.optimization_barrier(jnp.sum(unit * upstream, axis=-1, keepdims=True)))

def pair_terms(queries, keys, temper, offset, paired):
    sims = lax.dot_general(queries, keys, (((1,), (1,)), ((), ())), preferred_element_type=jnp.float32)
    logits = temper * sims + offset
    label = paired.astype(jnp.float32)
    loss_part = jnp.sum(jax.nn.softplus(-(2.0 * label - 1.0) * logits))
    coeff = jax.nn.sigmoid(logits) - label
    return (loss_part, jnp.sum(coeff * temper * sims), jnp.sum(coeff), coeff.astype(jnp.bfloat16))

def key_partial(coeff_low, queries):
    return lax.dot_general(coeff_low, queries, (((0,), (0,)), ((), ())), preferred_element_type=jnp.float32)

def reference(images, captions, pair_index, logit_scale, logit_bias):
    unit_img, inv_img = normalize(images)
    unit_cap, inv_cap = normalize(captions)
    query_all = unit_img.astype(jnp.bfloat16)
    key_all = unit_cap.astype(jnp.bfloat16)
    temper = jnp.exp(logit_scale[0])
    offset = logit_bias[0]
    query_blocks = query_all.reshape(N_BLK, BLOCK, E)
    key_blocks = key_all.reshape(N_BLK, BLOCK, E)
    windowed = jnp.stack([jnp.roll(key_blocks, k, axis=0) for k in range(WINDOW)], axis=1)
    columns = jnp.arange(BLOCK, dtype=jnp.int32)

    def per_block(pieces):
        queries, keys, match_rows = pieces
        image_grad = jnp.zeros((BLOCK, E), jnp.float32)
        loss_total = jnp.zeros((), jnp.float32)
        scale_total = jnp.zeros((), jnp.float32)
        bias_total = jnp.zeros((), jnp.float32)
        partials = []
        for k in range(WINDOW):
            if k == 0:
                paired = columns[None, :] == match_rows[:, None]
            else:
                paired = jnp.zeros((BLOCK, BLOCK), bool)
            loss_part, scale_part, bias_part, coeff_low = pair_terms(queries, keys[k], temper, offset, paired)
            loss_total = loss_total + loss_part
            scale_total = scale_total + scale_part
            bias_total = bias_total + bias_part
            image_grad = image_grad + jnp.dot(coeff_low, keys[k], preferred_element_type=jnp.float32)
            partials.append(temper * key_partial(coeff_low, queries))
        return (temper * image_grad, jnp.stack(partials), loss_total, scale_total, bias_total)
    image_grad, partials, losses, scale_parts, bias_parts = lax.map(per_block, (query_blocks, windowed, pair_index))
    caption_grad = partials[:, 0]
    for k in range(1, WINDOW):
        caption_grad = caption_grad + jnp.roll(partials[:, k], -k, axis=0)
    pair_count = TOTAL * WINDOW * BLOCK
    grad_images = backnorm(unit_img, inv_img, image_grad.reshape(TOTAL, E))
    grad_captions = backnorm(unit_cap, inv_cap, caption_grad.reshape(TOTAL, E))
    loss_mean = (jnp.sum(losses) / pair_count).reshape(1)
    grad_scale = (jnp.sum(scale_parts) / pair_count).reshape(1)
    grad_bias = (jnp.sum(bias_parts) / pair_count).reshape(1)
    return (loss_mean, grad_images, grad_captions, grad_scale, grad_bias)
```

```python
import functools

import jax
import jax.numpy as jnp
from jax import lax
from jax.experimental import pallas as pl
from jax.experimental.pallas import tpu as pltpu
from jax.sharding import PartitionSpec as P

MESH = pl.DeviceIdType.MESH
EPS = 1e-06
WINDOW = 2
NX = 4
ROWS = 128
E = 1152
LANES = 128

M_Q = 0
M_PI = 3
M_KSIB0, M_KY, M_KSIB1 = 6, 7, 8
M_KZ, M_KD, M_LSIB0, M_LSIB1 = 9, 10, 11, 12
M_DQ = 13
M_DQS = 16
M_SS = 19
M_Z, M_ZS, M_D, M_DS, M_Y, M_YS = 21, 22, 23, 24, 25, 26
M_ST = 27
N_MSG = 27 + 21


def kernel(n_blk, im_ref, cap_ref, pi_ref, ls_ref, lb_ref,
           loss_ref, gi_ref, gc_ref, gs_ref, gb_ref,
           Q, PI, K, C, S, INV, ACCQ, ACCK, SS, RS,
           SQ, SQS, RQ, RQS, SK, SKS, RK, RKS, ST, RT, SUMS,
           ssem, rsem):
    b = lax.axis_index("blk")
    g = lax.axis_index("gather")
    core = lax.rem(g, 2)
    x = lax.rem(g // 2, NX)
    yh = g // (2 * NX)
    nz = n_blk // 2
    zl_n = min(4, nz)
    zh_n = nz // zl_n
    z = lax.rem(b, nz)
    yl = b // nz
    zl = lax.rem(z, zl_n)
    zh = z // zl_n

    def gat(yh_, x_, core_):
        return yh_ * (2 * NX) + lax.rem(x_, NX) * 2 + core_

    def blk(yl_, zh_, zl_):
        return yl_ * nz + zh_ * zl_n + zl_

    g_off = [g, gat(yh, x + 2, core), gat(yh, x + 1, core), gat(yh, x + 3, core)]
    back = [0, 1, 3, 2]
    g_y = gat(1 - yh, x, core)
    b_n = lax.rem(b + 1, n_blk)
    b_p = lax.rem(b + n_blk - 1, n_blk)
    sib = (b, gat(yh, x, 1 - core))
    y_peer = (b, g_y)
    stage1 = []
    for i in range(1, 8):
        j = lax.rem(lax.rem(g, 8) + i, 8)
        stage1.append((b, yh * 8 + j))
    n2, n3 = 2 * zl_n, 2 * zh_n
    stage2 = []
    for i in range(1, n2):
        j = lax.rem(yh * zl_n + zl + i, n2)
        stage2.append((blk(yl, zh, lax.rem(j, zl_n)), gat(j // zl_n, x, core)))
    stage3 = []
    for i in range(1, n3):
        j = lax.rem(yl * zh_n + zh + i, n3)
        stage3.append((blk(j // zh_n, lax.rem(j, zh_n), zl), g))
    near = [(b_n, g), (b_p, g), (b_n, g_y), (b_p, g_y)]

    barrier = pltpu.get_barrier_semaphore()
    greeted = stage1 + stage2 + stage3 + near
    for peer in greeted:
        pl.semaphore_signal(barrier, inc=1, device_id=peer, device_id_type=MESH)

    def copy(m, src, dst, peer):
        return pltpu.make_async_remote_copy(
            src_ref=src, dst_ref=dst, send_sem=ssem.at[m], recv_sem=rsem.at[m],
            device_id=peer, device_id_type=MESH)

    temper = jnp.exp(jnp.full((1, LANES), ls_ref[0], jnp.float32))
    bias = lb_ref[0]
    PI[0] = jnp.broadcast_to(pi_ref[...], (8, LANES))

    def normalize(src, dst, which):
        def body(i, _):
            rows = pl.ds(pl.multiple_of(i * 16, 16), 16)
            v = src[rows, :].astype(jnp.float32)
            inv = lax.rsqrt(jnp.sum(v * v, axis=1, keepdims=True) + EPS)
            INV[which, rows, :] = jnp.broadcast_to(inv, (16, LANES))
            dst[rows, :] = (v * inv).astype(jnp.bfloat16)
            return 0
        lax.fori_loop(0, ROWS // 16, body, 0)

    normalize(im_ref, Q.at[0], 0)
    normalize(cap_ref, K.at[0, 0], 1)

    pl.semaphore_wait(barrier, len(greeted))

    sent = []

    def send(m, src, dst, peer):
        c = copy(m, src, dst, peer)
        c.start()
        sent.append(c)
        return c

    for s in (2, 3, 1):
        send(M_PI + s - 1, PI.at[0], PI.at[back[s]], (b, g_off[s]))
    for s in (2, 3, 1):
        send(M_Q + s - 1, Q.at[0], Q.at[back[s]], (b, g_off[s]))
    send(M_KY, K.at[0, 0], K.at[0, 1], y_peer)
    send(M_KZ, K.at[0, 0], K.at[1, 0], (b_n, g))
    send(M_KSIB0, K.at[0, 0], K.at[0, 2], sib)
    send(M_KD, K.at[0, 0], K.at[1, 1], (b_n, g_y))

    def arrived(m, dst):
        copy(m, dst, dst, sib).wait_recv()

    arrived(M_KY, K.at[0, 1])
    send(M_KSIB1, K.at[0, 1], K.at[0, 3], sib)
    arrived(M_KZ, K.at[1, 0])
    send(M_LSIB0, K.at[1, 0], K.at[1, 2], sib)
    arrived(M_KD, K.at[1, 1])
    send(M_LSIB1, K.at[1, 1], K.at[1, 3], sib)

    arrived(M_KSIB0, K.at[0, 2])
    arrived(M_KSIB1, K.at[0, 3])
    for s in (2, 3, 1):
        arrived(M_PI + back[s] - 1, PI.at[s])
        arrived(M_Q + back[s] - 1, Q.at[s])
    arrived(M_LSIB0, K.at[1, 2])
    arrived(M_LSIB1, K.at[1, 3])

    temper2 = jnp.concatenate([temper, temper], axis=1)
    k_base = [gat(yh, x, core), g_y, gat(yh, x, 1 - core), gat(1 - yh, x, 1 - core)]
    SUMS[...] = jnp.zeros_like(SUMS)
    NT = (((1,), (1,)), ((), ()))
    TN = (((0,), (0,)), ((), ()))

    def pair_terms(k, h):
        q2 = Q[2 * h:2 * h + 2].reshape(2 * ROWS, E)
        keys = K[k].reshape(4 * ROWS, E)
        S[...] = lax.dot_general(keys, q2, NT, preferred_element_type=jnp.float32)
        cols = slice(2 * h * ROWS, (2 * h + 2) * ROWS)
        pair = jnp.concatenate([PI[2 * h, 0:1], PI[2 * h + 1, 0:1]], axis=1)
        for t in range(4):
            def body(i, tot):
                rows = pl.ds(pl.multiple_of(t * ROWS + i * 32, 32), 32)
                ts = temper2 * S[rows, :]
                logits = ts + bias
                p = jnp.exp(logits)
                d = 1.0 + p
                coeff = p / d
                prod = (d[0:8] * d[8:16]) * (d[16:24] * d[24:32])
                loss = jnp.log(prod)
                if k == 0:
                    cid = lax.broadcasted_iota(jnp.int32, (32, 2 * ROWS), 0) + (k_base[t] * ROWS + i * 32)
                    hit = cid == pair
                    coeff = jnp.where(hit, coeff - 1.0, coeff)
                    own = jnp.where(hit, logits, 0.0)
                    loss = loss - ((own[0:8] + own[8:16]) + (own[16:24] + own[24:32]))
                sc = coeff * ts
                C[k, rows, cols] = coeff.astype(jnp.bfloat16)
                fold = lambda v: (v[0:8] + v[8:16]) + (v[16:24] + v[24:32])
                return tot[0] + loss, tot[1] + fold(sc), tot[2] + fold(coeff)
            zero = jnp.zeros((8, 2 * ROWS), jnp.float32)
            tot = lax.fori_loop(0, ROWS // 32, body, (zero, zero, zero))
            for j in range(3):
                SUMS[j] += tot[j]

    for h in range(2):
        for k in range(WINDOW):
            pair_terms(k, h)

    row = lax.broadcasted_iota(jnp.int32, (8, LANES), 0)
    mine = jnp.zeros((8, LANES), jnp.float32)
    for j in range(3):
        v = jnp.sum(SUMS[j], axis=0, keepdims=True)
        v = v[:, 0:LANES] + v[:, LANES:]
        mine = jnp.where(row == j, v, mine)
    ST[0] = mine
    for i, peer in enumerate(stage1):
        send(M_ST + i, ST.at[0], RT.at[0, i], peer)

    def quantize(src, srow, dst, dst_scale):
        def body(j, _):
            cs = pl.ds(pl.multiple_of(j * LANES, LANES), LANES)
            v = src[srow:srow + ROWS, cs]
            m = jnp.max(jnp.abs(v), axis=0, keepdims=True)
            up = 32767.0 / jnp.maximum(m, 1e-30)
            dst[:, cs] = jnp.round(v * up).astype(jnp.int32).astype(jnp.int16)
            dst_scale[:, cs] = m * (1.0 / 32767.0)
            return 0
        lax.fori_loop(0, E // LANES, body, 0)

    def image_part(h):
        cols = slice(2 * h * ROWS, (2 * h + 2) * ROWS)
        ACCQ[h] = (
            lax.dot_general(C[0, :, cols], K[0].reshape(4 * ROWS, E), TN, preferred_element_type=jnp.float32)
            + lax.dot_general(C[1, :, cols], K[1].reshape(4 * ROWS, E), TN, preferred_element_type=jnp.float32))

    def send_image(s):
        quantize(ACCQ.at[s // 2], (s % 2) * ROWS, SQ.at[s - 1], SQS.at[s - 1])
        send(M_DQ + s - 1, SQ.at[s - 1], RQ.at[back[s] - 1], (b, g_off[s]))
        send(M_DQS + s - 1, SQS.at[s - 1], RQS.at[back[s] - 1], (b, g_off[s]))

    def key_part(k, half):
        return jnp.dot(C[k, half * 256:half * 256 + 256, :], Q[...].reshape(4 * ROWS, E),
                       preferred_element_type=jnp.float32)

    SS[1] = key_part(1, 1)
    send(M_SS + 1, SS.at[1], RS.at[1], sib)
    image_part(1)
    send_image(2)
    send_image(3)
    ACCK[1] = key_part(1, 0)
    arrived(M_SS + 1, RS.at[1])

    def add_rs(k):
        def body(i, _):
            rows = pl.ds(pl.multiple_of(i * 16, 16), 16)
            ACCK[k, rows, :] += RS[k, rows, :]
            return 0
        lax.fori_loop(0, 2 * ROWS // 16, body, 0)

    def send_key(i, k, half, m, peer):
        quantize(ACCK.at[k], half * ROWS, SK.at[i], SKS.at[i])
        send(m, SK.at[i], RK.at[i], peer)
        send(m + 1, SKS.at[i], RKS.at[i], peer)

    add_rs(1)
    send_key(1, 1, 1, M_D, (b_p, g_y))
    send_key(0, 1, 0, M_Z, (b_p, g))
    image_part(0)
    send_image(1)
    SS[0] = key_part(0, 1)
    send(M_SS, SS.at[0], RS.at[0], sib)
    ACCK[0] = key_part(0, 0)
    arrived(M_SS, RS.at[0])
    add_rs(0)
    send_key(2, 0, 1, M_Y, y_peer)

    def gather_stage(st, peers, base):
        tot = ST[st]
        for i in range(len(peers)):
            arrived(M_ST + base + i, RT.at[st, i])
            tot = tot + RT[st, i]
        return tot

    tot = gather_stage(0, stage1, 0)
    ST[1] = tot
    for i, peer in enumerate(stage2):
        send(M_ST + 7 + i, ST.at[1], RT.at[1, i], peer)
    tot = gather_stage(1, stage2, 7)
    ST[2] = tot
    for i, peer in enumerate(stage3):
        send(M_ST + 14 + i, ST.at[2], RT.at[2, i], peer)
    tot = gather_stage(2, stage3, 14)
    count = 1.0 / (n_blk * WINDOW * 2048.0 * 2048.0)
    for j, ref in ((0, loss_ref), (1, gs_ref), (2, gb_ref)):
        ref[0] = jnp.sum(tot[j:j + 1, :]) * count

    def finish(src, which, own, parts, out):
        def body(i, _):
            rows = pl.ds(pl.multiple_of(i * 16, 16), 16)
            inv = INV[which, rows, 0:1]
            unit = src[rows, :].astype(jnp.float32) * inv
            grad = own[rows, :]
            for data, scale in parts:
                grad = grad + data[rows, :].astype(jnp.int32).astype(jnp.float32) * scale[...]
            grad = grad * temper[:, 0:1]
            along = jnp.sum(unit * grad, axis=1, keepdims=True)
            out[rows, :] = inv * (grad - unit * along)
            return 0
        lax.fori_loop(0, ROWS // 16, body, 0)

    for s in (2, 3, 1):
        arrived(M_DQ + back[s] - 1, RQ.at[s - 1])
        arrived(M_DQS + back[s] - 1, RQS.at[s - 1])
    finish(im_ref, 0, ACCQ.at[0], [(RQ.at[i], RQS.at[i]) for i in range(3)], gi_ref)
    for i, m in enumerate((M_Z, M_D, M_Y)):
        arrived(m, RK.at[i])
        arrived(m + 1, RKS.at[i])
    finish(cap_ref, 1, ACCK.at[0], [(RK.at[i], RKS.at[i]) for i in range(3)], gc_ref)
    for c in sent:
        c.wait_send()


def on_device(n_blk, images, captions, pair_index, logit_scale, logit_bias):
    vmem = pl.BlockSpec(memory_space=pltpu.VMEM)
    smem = pl.BlockSpec(memory_space=pltpu.SMEM)
    f32, bf16, i16 = jnp.float32, jnp.bfloat16, jnp.int16
    one = jax.ShapeDtypeStruct((1,), f32)
    grad = jax.ShapeDtypeStruct((ROWS, E), f32)
    unit = (ROWS, E)
    return pl.pallas_call(
        functools.partial(kernel, n_blk),
        out_shape=(one, grad, grad, one, one),
        in_specs=[vmem, vmem, vmem, smem, smem],
        out_specs=(smem, vmem, vmem, smem, smem),
        scratch_shapes=[
            pltpu.VMEM((4,) + unit, bf16),
            pltpu.VMEM((4, 8, LANES), jnp.int32),
            pltpu.VMEM((2, 4) + unit, bf16),
            pltpu.VMEM((2, 512, 512), bf16),
            pltpu.VMEM((512, 256), f32),
            pltpu.VMEM((2, ROWS, LANES), f32),
            pltpu.VMEM((2, 2 * ROWS, E), f32),
            pltpu.VMEM((2, 2 * ROWS, E), f32),
            pltpu.VMEM((2, 2 * ROWS, E), f32),
            pltpu.VMEM((2, 2 * ROWS, E), f32),
            pltpu.VMEM((3,) + unit, i16),
            pltpu.VMEM((3, 1, E), f32),
            pltpu.VMEM((3,) + unit, i16),
            pltpu.VMEM((3, 1, E), f32),
            pltpu.VMEM((3,) + unit, i16),
            pltpu.VMEM((3, 1, E), f32),
            pltpu.VMEM((3,) + unit, i16),
            pltpu.VMEM((3, 1, E), f32),
            pltpu.VMEM((3, 8, LANES), f32),
            pltpu.VMEM((3, 7, 8, LANES), f32),
            pltpu.VMEM((3, 8, 2 * LANES), f32),
            pltpu.SemaphoreType.DMA((N_MSG,)),
            pltpu.SemaphoreType.DMA((N_MSG,)),
        ],
        compiler_params=pltpu.CompilerParams(
            collective_id=0, has_side_effects=True, vmem_limit_bytes=48 * 2**20),
    )(images, captions, pair_index, logit_scale, logit_bias)


def solution(mesh):
    placed = (P(("blk", "gather"), None), P(("blk", "gather"), None), P("blk", "gather"), P(), P())
    return jax.shard_map(
        functools.partial(on_device, mesh.shape["blk"]),
        mesh=mesh,
        in_specs=placed,
        out_specs=(P(), P(("blk", "gather"), None), P(("blk", "gather"), None), P(), P()),
        check_vma=False,
    )
```

```python
import functools

import jax
import jax.numpy as jnp
from jax import lax
from jax.experimental import pallas as pl
from jax.experimental.pallas import tpu as pltpu
from jax.sharding import PartitionSpec as P

MESH = pl.DeviceIdType.MESH
EPS = 1e-06
WINDOW = 2
NX = 4
ROWS = 128
E = 1152
LANES = 128

H = ROWS // 2

MESSAGES = [
    "QRa", "QRb", "QLb", "QLa", "QFR", "QFL", "PIR", "PIL", "PIO",
    "KYa", "KYb", "KZa", "KZb", "KS", "FZ", "FY", "S0a", "S0b", "S1a", "S1b", "S2a", "S2b",
    "XOa", "XOb", "XRa", "XRb", "XLa", "XLb", "Y1a", "Y0a", "Y0b", "Z1b", "Zob", "Zoa",
    "G1", "G0",
] + ["T%d%d" % (i, j) for i in range(3) for j in range(7)]
PARTS = ["XOa", "XOb", "XRa", "XRb", "XLa", "XLb", "Y1a", "Y0a", "Y0b", "Z1b", "Zob", "Zoa"]
SCALES = len(MESSAGES)
N_MSG = SCALES + len(PARTS)


def kernel(n_blk, im_hbm, cap_hbm, pi_ref, ls_ref, lb_ref,
           loss_ref, gi_ref, gc_ref, gs_ref, gb_ref,
           IM, CAP, Q, PI, K, C, INV, ACCQ, ACCK, SS, RS,
           SP, SPS, RP, RPS, ST, RT, SUMS, isem, ssem, rsem):
    b = lax.axis_index("blk")
    g = lax.axis_index("gather")
    core = lax.rem(g, 2)
    x = lax.rem(g // 2, NX)
    yh = g // (2 * NX)
    nz = n_blk // 2
    zl_n = min(4, nz)
    zh_n = nz // zl_n
    z = lax.rem(b, nz)
    yl = b // nz
    zl = lax.rem(z, zl_n)
    zh = z // zl_n

    def gat(yh_, x_, core_):
        return yh_ * (2 * NX) + lax.rem(x_, NX) * 2 + core_

    def blk(yl_, zh_, zl_):
        return yl_ * nz + zh_ * zl_n + zl_

    g_y = gat(1 - yh, x, core)
    right = (b, gat(yh, x + 1, core))
    left = (b, gat(yh, x + 3, core))
    opposite = (b, gat(yh, x + 2, core))
    b_n = lax.rem(b + 1, n_blk)
    b_p = lax.rem(b + n_blk - 1, n_blk)
    sib = (b, gat(yh, x, 1 - core))
    y_peer = (b, g_y)
    z_next = (b_n, g)
    z_prev = (b_p, g)
    stage1 = []
    for i in range(1, 8):
        j = lax.rem(lax.rem(g, 8) + i, 8)
        stage1.append((b, yh * 8 + j))
    n2, n3 = 2 * zl_n, 2 * zh_n
    stage2 = []
    for i in range(1, n2):
        j = lax.rem(yh * zl_n + zl + i, n2)
        stage2.append((blk(yl, zh, lax.rem(j, zl_n)), gat(j // zl_n, x, core)))
    stage3 = []
    for i in range(1, n3):
        j = lax.rem(yl * zh_n + zh + i, n3)
        stage3.append((blk(j // zh_n, lax.rem(j, zh_n), zl), g))

    barrier = pltpu.get_barrier_semaphore()
    greeted = stage1 + stage2 + stage3 + [z_next, z_prev]
    for peer in greeted:
        pl.semaphore_signal(barrier, inc=1, device_id=peer, device_id_type=MESH)

    fetch = [pltpu.make_async_copy(im_hbm, IM, isem.at[0]), pltpu.make_async_copy(cap_hbm, CAP, isem.at[1])]
    for f in fetch:
        f.start()

    temper = jnp.exp(jnp.full((1, LANES), ls_ref[0], jnp.float32))
    bias = lb_ref[0]
    PI[0] = jnp.broadcast_to(pi_ref[...], (8, LANES))
    SUMS[...] = jnp.zeros_like(SUMS)

    def normalize(src, dst, which):
        def body(i, _):
            rows = pl.ds(pl.multiple_of(i * 16, 16), 16)
            v = src[rows, :].astype(jnp.float32)
            inv = lax.rsqrt(jnp.sum(v * v, axis=1, keepdims=True) + EPS)
            INV[which, rows, :] = jnp.broadcast_to(inv, (16, LANES))
            dst[rows, :] = (v * inv).astype(jnp.bfloat16)
            return 0
        lax.fori_loop(0, ROWS // 16, body, 0, unroll=4)

    sent = []

    def copy(m, src, dst, peer):
        return pltpu.make_async_remote_copy(
            src_ref=src, dst_ref=dst, send_sem=ssem.at[m], recv_sem=rsem.at[m],
            device_id=peer, device_id_type=MESH)

    def send(name, src, dst, peer):
        m = name if isinstance(name, int) else MESSAGES.index(name)
        c = copy(m, src, dst, peer)
        c.start()
        sent.append(c)

    def arrived(name, dst):
        m = name if isinstance(name, int) else MESSAGES.index(name)
        copy(m, dst, dst, sib).wait_recv()

    a_half, b_half = pl.ds(0, H), pl.ds(H, H)
    OWN, LEFT, RIGHT, OPP = range(4)
    SIB, YP, YS = 1, 2, 3

    fetch[0].wait()
    normalize(IM, Q.at[OWN], 0)
    pl.semaphore_wait(barrier, len(greeted))
    send("PIR", PI.at[OWN], PI.at[LEFT], right)
    send("PIL", PI.at[OWN], PI.at[RIGHT], left)
    send("PIO", PI.at[OWN], PI.at[OPP], opposite)
    send("QRa", Q.at[OWN, a_half], Q.at[LEFT, a_half], right)
    send("QLb", Q.at[OWN, b_half], Q.at[RIGHT, b_half], left)
    send("QRb", Q.at[OWN, b_half], Q.at[LEFT, b_half], right)
    send("QLa", Q.at[OWN, a_half], Q.at[RIGHT, a_half], left)
    fetch[1].wait()
    normalize(CAP, K.at[0, OWN], 1)
    send("KYa", K.at[0, OWN, a_half], K.at[0, YP, a_half], y_peer)
    send("KZb", K.at[0, OWN, b_half], K.at[1, OWN, b_half], z_next)
    send("KYb", K.at[0, OWN, b_half], K.at[0, YP, b_half], y_peer)
    send("KZa", K.at[0, OWN, a_half], K.at[1, OWN, a_half], z_next)
    send("KS", K.at[0, OWN], K.at[0, SIB], sib)

    own_base = [gat(yh, x, core), gat(yh, x, 1 - core), g_y, gat(1 - yh, x, 1 - core)]
    NT = (((1,), (1,)), ((), ()))
    TN = (((0,), (0,)), ((), ()))

    def fold(v):
        return (v[0:8] + v[8:16]) + (v[16:24] + v[24:32])

    def pair_terms(k, kp, s):
        keys = K[k, 2 * kp:2 * kp + 2].reshape(2 * ROWS, E)
        sims = lax.dot_general(keys, Q[s], NT, preferred_element_type=jnp.float32)
        cols = slice(s * ROWS, (s + 1) * ROWS)
        tot = None
        for i in range(8):
            ts = temper * sims[i * 32:(i + 1) * 32]
            logits = ts + bias
            p = jnp.exp(logits)
            d = 1.0 + p
            coeff = p / d
            prod = (d[0:8] * d[8:16]) * (d[16:24] * d[24:32])
            loss = jnp.log(prod)
            t = 2 * kp + i // 4
            if k == 0:
                cid = lax.broadcasted_iota(jnp.int32, (32, ROWS), 0) + (own_base[t] * ROWS + (i % 4) * 32)
                hit = cid == PI[s, 0:1]
                coeff = jnp.where(hit, coeff - 1.0, coeff)
                loss = loss - fold(jnp.where(hit, logits, 0.0))
            C[k, t, (i % 4) * 32:(i % 4) * 32 + 32, cols] = coeff.astype(jnp.bfloat16)
            new = (loss, fold(coeff * ts), fold(coeff))
            tot = new if tot is None else tuple(u + v for u, v in zip(tot, new))
        for j in range(3):
            SUMS[j] += tot[j]

    arrived("KS", K.at[0, SIB])
    pair_terms(0, 0, OWN)

    arrived("QRa", Q.at[LEFT, a_half])
    send("QFR", Q.at[LEFT, a_half], Q.at[OPP, a_half], right)
    arrived("QLb", Q.at[RIGHT, b_half])
    send("QFL", Q.at[RIGHT, b_half], Q.at[OPP, b_half], left)
    arrived("KYa", K.at[0, YP, a_half])
    send("FZ", K.at[0, YP, a_half], K.at[1, YP, a_half], z_next)
    send("S0a", K.at[0, YP, a_half], K.at[0, YS, a_half], sib)
    arrived("KZb", K.at[1, OWN, b_half])
    send("FY", K.at[1, OWN, b_half], K.at[1, YP, b_half], y_peer)
    send("S1b", K.at[1, OWN, b_half], K.at[1, SIB, b_half], sib)
    arrived("KYb", K.at[0, YP, b_half])
    send("S0b", K.at[0, YP, b_half], K.at[0, YS, b_half], sib)
    arrived("KZa", K.at[1, OWN, a_half])
    send("S1a", K.at[1, OWN, a_half], K.at[1, SIB, a_half], sib)
    arrived("QRb", Q.at[LEFT, b_half])
    arrived("QLa", Q.at[RIGHT, a_half])
    arrived("PIR", PI.at[LEFT])
    arrived("PIL", PI.at[RIGHT])
    pair_terms(0, 0, LEFT)
    pair_terms(0, 0, RIGHT)
    arrived("S0a", K.at[0, YS, a_half])
    arrived("S0b", K.at[0, YS, b_half])
    for s in (OWN, LEFT, RIGHT):
        pair_terms(0, 1, s)
    arrived("FZ", K.at[1, YP, a_half])
    send("S2a", K.at[1, YP, a_half], K.at[1, YS, a_half], sib)
    arrived("FY", K.at[1, YP, b_half])
    send("S2b", K.at[1, YP, b_half], K.at[1, YS, b_half], sib)
    arrived("S1b", K.at[1, SIB, b_half])
    arrived("S1a", K.at[1, SIB, a_half])
    for s in (OWN, LEFT, RIGHT):
        pair_terms(1, 0, s)
    arrived("PIO", PI.at[OPP])
    arrived("QFR", Q.at[OPP, a_half])
    arrived("QFL", Q.at[OPP, b_half])
    pair_terms(1, 0, OPP)
    arrived("S2a", K.at[1, YS, a_half])
    arrived("S2b", K.at[1, YS, b_half])
    for s in (OWN, LEFT, RIGHT, OPP):
        pair_terms(1, 1, s)

    def key_part(k, slots):
        coeff = jnp.concatenate([C[k, t] for t in slots], axis=0)
        return jnp.dot(coeff, Q[...].reshape(4 * ROWS, E), preferred_element_type=jnp.float32)

    def image_part(slots):
        cols = slice(slots[0] * ROWS, (slots[-1] + 1) * ROWS)
        out = None
        for k in range(WINDOW):
            new = lax.dot_general(C[k, :, :, cols].reshape(4 * ROWS, -1), K[k].reshape(4 * ROWS, E), TN,
                                  preferred_element_type=jnp.float32)
            out = new if out is None else out + new
        for i, s in enumerate(slots):
            ACCQ[s] = out[i * ROWS:(i + 1) * ROWS]

    def part(name, terms, peer):
        p = PARTS.index(name)
        def body(j, _):
            cs = pl.ds(pl.multiple_of(j * LANES, LANES), LANES)
            v = None
            for t in terms:
                if isinstance(t, str):
                    q = PARTS.index(t)
                    u = RP[q, :, cs].astype(jnp.int32).astype(jnp.float32) * RPS[q, :, cs]
                else:
                    u = t[0][t[1], cs]
                v = u if v is None else v + u
            m = jnp.max(jnp.abs(v), axis=0, keepdims=True)
            up = 32767.0 / jnp.maximum(m, 1e-30)
            SP[p, :, cs] = jnp.round(v * up).astype(jnp.int32).astype(jnp.int16)
            SPS[p, :, cs] = m * (1.0 / 32767.0)
            return 0
        lax.fori_loop(0, E // LANES, body, 0, unroll=3)
        send(name, SP.at[p], RP.at[p], peer)
        send(SCALES + p, SPS.at[p], RPS.at[p], peer)

    def part_in(name):
        p = PARTS.index(name)
        arrived(name, RP.at[p])
        arrived(SCALES + p, RPS.at[p])

    SS[1] = key_part(1, (SIB, YS))
    send("G1", SS.at[1], RS.at[1], sib)
    pair_terms(0, 0, OPP)
    pair_terms(0, 1, OPP)

    row = lax.broadcasted_iota(jnp.int32, (8, LANES), 0)
    mine = jnp.zeros((8, LANES), jnp.float32)
    for j in range(3):
        mine = jnp.where(row == j, jnp.sum(SUMS[j], axis=0, keepdims=True), mine)
    ST[0] = mine
    for i, peer in enumerate(stage1):
        send("T0%d" % i, ST.at[0], RT.at[0, i], peer)

    def stage_sum(st, peers):
        tot = ST[st]
        for i in range(len(peers)):
            arrived("T%d%d" % (st, i), RT.at[st, i])
            tot = tot + RT[st, i]
        return tot

    image_part((OPP,))
    part("XOa", [(ACCQ.at[OPP], a_half)], right)
    part("XOb", [(ACCQ.at[OPP], b_half)], left)
    ACCK[1] = key_part(1, (OWN, YP))
    arrived("G1", RS.at[1])
    own_a, own_b, y_a, y_b = pl.ds(0, H), pl.ds(H, H), pl.ds(2 * H, H), pl.ds(3 * H, H)
    part("Y1a", [(ACCK.at[1], y_a), (RS.at[1], y_a)], y_peer)
    part("Z1b", [(ACCK.at[1], y_b), (RS.at[1], y_b)], z_prev)
    SS[0] = key_part(0, (SIB, YS))
    send("G0", SS.at[0], RS.at[0], sib)
    image_part((LEFT, RIGHT))
    part("XRb", [(ACCQ.at[RIGHT], b_half)], right)
    part("XLa", [(ACCQ.at[LEFT], a_half)], left)
    part("Zob", [(ACCK.at[1], own_b), (RS.at[1], own_b)], z_prev)
    ACCK[0] = key_part(0, (OWN, YP))
    arrived("G0", RS.at[0])
    part("Y0a", [(ACCK.at[0], y_a), (RS.at[0], y_a)], y_peer)

    ST[1] = stage_sum(0, stage1)
    for i, peer in enumerate(stage2):
        send("T1%d" % i, ST.at[1], RT.at[1, i], peer)

    part_in("XOa")
    part("XRa", [(ACCQ.at[RIGHT], a_half), "XOa"], right)
    part_in("XOb")
    part("XLb", [(ACCQ.at[LEFT], b_half), "XOb"], left)
    part_in("Y1a")
    part("Zoa", [(ACCK.at[1], own_a), (RS.at[1], own_a), "Y1a"], z_prev)
    part_in("Z1b")
    part("Y0b", [(ACCK.at[0], y_b), (RS.at[0], y_b), "Z1b"], y_peer)
    image_part((OWN,))

    ST[2] = stage_sum(1, stage2)
    for i, peer in enumerate(stage3):
        send("T2%d" % i, ST.at[2], RT.at[2, i], peer)

    def finish(half, src, which, own, parts, out):
        def body(i, _):
            local = pl.ds(pl.multiple_of(i * 16, 16), 16)
            rows = pl.ds(pl.multiple_of(half * H + i * 16, 16), 16)
            inv = INV[which, rows, 0:1]
            unit = src[rows, :].astype(jnp.float32) * inv
            grad = None
            for o in own:
                grad = o[rows, :] if grad is None else grad + o[rows, :]
            for name in parts:
                q = PARTS.index(name)
                grad = grad + RP[q, local, :].astype(jnp.int32).astype(jnp.float32) * RPS[q]
            grad = grad * temper[:, 0:1]
            along = jnp.sum(unit * grad, axis=1, keepdims=True)
            out[rows, :] = inv * (grad - unit * along)
            return 0
        lax.fori_loop(0, H // 16, body, 0, unroll=2)

    key_own = [ACCK.at[0], RS.at[0]]
    part_in("XRb")
    part_in("XLb")
    finish(1, IM, 0, [ACCQ.at[OWN]], ["XRb", "XLb"], gi_ref)
    part_in("XRa")
    part_in("XLa")
    finish(0, IM, 0, [ACCQ.at[OWN]], ["XRa", "XLa"], gi_ref)
    part_in("Zoa")
    part_in("Y0a")
    finish(0, CAP, 1, key_own, ["Zoa", "Y0a"], gc_ref)
    part_in("Zob")
    part_in("Y0b")
    finish(1, CAP, 1, key_own, ["Zob", "Y0b"], gc_ref)

    tot = stage_sum(2, stage3)
    count = 1.0 / (n_blk * WINDOW * 2048.0 * 2048.0)
    for j, ref in ((0, loss_ref), (1, gs_ref), (2, gb_ref)):
        ref[0] = jnp.sum(tot[j:j + 1, :]) * count
    for c in sent:
        c.wait_send()


def on_device(n_blk, images, captions, pair_index, logit_scale, logit_bias):
    vmem = pl.BlockSpec(memory_space=pltpu.VMEM)
    smem = pl.BlockSpec(memory_space=pltpu.SMEM)
    hbm = pl.BlockSpec(memory_space=pl.ANY)
    f32, bf16, i16 = jnp.float32, jnp.bfloat16, jnp.int16
    one = jax.ShapeDtypeStruct((1,), f32)
    grad = jax.ShapeDtypeStruct((ROWS, E), f32)
    unit = (ROWS, E)
    n = len(PARTS)
    return pl.pallas_call(
        functools.partial(kernel, n_blk),
        out_shape=(one, grad, grad, one, one),
        in_specs=[hbm, hbm, vmem, smem, smem],
        out_specs=(smem, vmem, vmem, smem, smem),
        scratch_shapes=[
            pltpu.VMEM(unit, bf16),
            pltpu.VMEM(unit, bf16),
            pltpu.VMEM((4,) + unit, bf16),
            pltpu.VMEM((4, 8, LANES), jnp.int32),
            pltpu.VMEM((2, 4) + unit, bf16),
            pltpu.VMEM((2, 4, ROWS, 4 * ROWS), bf16),
            pltpu.VMEM((2, ROWS, LANES), f32),
            pltpu.VMEM((4,) + unit, f32),
            pltpu.VMEM((2, 2 * ROWS, E), f32),
            pltpu.VMEM((2, 2 * ROWS, E), f32),
            pltpu.VMEM((2, 2 * ROWS, E), f32),
            pltpu.VMEM((n, H, E), i16),
            pltpu.VMEM((n, 1, E), f32),
            pltpu.VMEM((n, H, E), i16),
            pltpu.VMEM((n, 1, E), f32),
            pltpu.VMEM((3, 8, LANES), f32),
            pltpu.VMEM((3, 7, 8, LANES), f32),
            pltpu.VMEM((3, 8, LANES), f32),
            pltpu.SemaphoreType.DMA((2,)),
            pltpu.SemaphoreType.DMA((N_MSG,)),
            pltpu.SemaphoreType.DMA((N_MSG,)),
        ],
        compiler_params=pltpu.CompilerParams(
            collective_id=0, has_side_effects=True, vmem_limit_bytes=48 * 2**20),
    )(images, captions, pair_index, logit_scale, logit_bias)


def solution(mesh):
    placed = (P(("blk", "gather"), None), P(("blk", "gather"), None), P("blk", "gather"), P(), P())
    return jax.shard_map(
        functools.partial(on_device, mesh.shape["blk"]),
        mesh=mesh,
        in_specs=placed,
        out_specs=(P(), P(("blk", "gather"), None), P(("blk", "gather"), None), P(), P()),
        check_vma=False,
    )
```

```python
import functools

import jax
import jax.numpy as jnp
from jax import lax
from jax.experimental import pallas as pl
from jax.experimental.pallas import tpu as pltpu
from jax.sharding import PartitionSpec as P

MESH = pl.DeviceIdType.MESH
EPS = 1e-06
WINDOW = 2
NX = 4
ROWS = 128
E = 1152
LANES = 128

H = ROWS // 2

MESSAGES = [
    "QRa", "QRb", "QLb", "QLa", "QFR", "QFL", "PIR", "PIL", "PIO",
    "KYa", "KYb", "KZa", "KZb", "KS", "FZ", "FY", "S0a", "S0b", "S1a", "S1b", "S2a", "S2b",
    "XOa", "XOb", "XRa", "XRb", "XLa", "XLb", "Y1a", "Y0a", "Y0b", "Z1b", "Zob", "Zoa",
    "G1y", "G1o", "G0y", "G0o", "DA", "DB", "Z1a", "EB",
] + ["T%d%d" % (i, j) for i in range(3) for j in range(7)]
PARTS = ["XOa", "XOb", "XRa", "XRb", "XLa", "XLb", "Y1a", "Y0a", "Y0b", "Z1b", "Zob", "Zoa", "DA", "DB", "Z1a"]
SCALES = len(MESSAGES)
N_MSG = SCALES + len(PARTS)


def kernel(n_blk, im_hbm, cap_hbm, pi_hbm, ls_ref, lb_ref,
           loss_ref, GI, GC, gs_ref, gb_ref,
           IM, CAP, PIN, Q, PI, K, C, INV, ACCQ, ACCK, SS, RS,
           SP, SPS, RP, RPS, ST, RT, SUMS, isem, ssem, rsem):
    b = lax.axis_index("blk")
    g = lax.axis_index("gather")
    core = lax.rem(g, 2)
    x = lax.rem(g // 2, NX)
    yh = g // (2 * NX)
    nz = n_blk // 2
    zl_n = min(4, nz)
    zh_n = nz // zl_n
    z = lax.rem(b, nz)
    yl = b // nz
    zl = lax.rem(z, zl_n)
    zh = z // zl_n

    def gat(yh_, x_, core_):
        return yh_ * (2 * NX) + lax.rem(x_, NX) * 2 + core_

    def blk(yl_, zh_, zl_):
        return yl_ * nz + zh_ * zl_n + zl_

    g_y = gat(1 - yh, x, core)
    right = (b, gat(yh, x + 1, core))
    left = (b, gat(yh, x + 3, core))
    opposite = (b, gat(yh, x + 2, core))
    b_n = lax.rem(b + 1, n_blk)
    b_p = lax.rem(b + n_blk - 1, n_blk)
    sib = (b, gat(yh, x, 1 - core))
    y_peer = (b, g_y)
    z_next = (b_n, g)
    z_prev = (b_p, g)
    first, last = z == 0, z == nz - 1
    not_first, not_last = z != 0, z != nz - 1
    inner = jnp.logical_and(not_first, not_last)
    before_last, not_before_last = z == nz - 2, z != nz - 2
    zy_next = (b_n, g_y)
    zy_prev = (b_p, g_y)
    stage1 = []
    for i in range(1, 8):
        j = lax.rem(lax.rem(g, 8) + i, 8)
        stage1.append((b, yh * 8 + j))
    n2, n3 = 2 * zl_n, 2 * zh_n
    stage2 = []
    for i in range(1, n2):
        j = lax.rem(yh * zl_n + zl + i, n2)
        stage2.append((blk(yl, zh, lax.rem(j, zl_n)), gat(j // zl_n, x, core)))
    stage3 = []
    for i in range(1, n3):
        j = lax.rem(yl * zh_n + zh + i, n3)
        stage3.append((blk(j // zh_n, lax.rem(j, zh_n), zl), g))

    barrier = pltpu.get_barrier_semaphore()
    greeted = stage1 + stage2 + stage3 + [z_next, z_prev, zy_next, zy_prev]
    for peer in greeted:
        pl.semaphore_signal(barrier, inc=1, device_id=peer, device_id_type=MESH)

    fetch = [pltpu.make_async_copy(im_hbm, IM, isem.at[0]), pltpu.make_async_copy(cap_hbm, CAP, isem.at[1]),
             pltpu.make_async_copy(pi_hbm, PIN, isem.at[2])]
    for f in fetch:
        f.start()

    temper = jnp.exp(jnp.full((1, LANES), ls_ref[0], jnp.float32))
    bias = lb_ref[0]
    SUMS[...] = jnp.zeros_like(SUMS)

    def normalize(src, dst, which):
        def body(i, _):
            rows = pl.ds(pl.multiple_of(i * 16, 16), 16)
            v = src[rows, :].astype(jnp.float32)
            inv = lax.rsqrt(jnp.sum(v * v, axis=1, keepdims=True) + EPS)
            INV[which, rows, :] = jnp.broadcast_to(inv, (16, LANES))
            dst[rows, :] = (v * inv).astype(jnp.bfloat16)
            return 0
        lax.fori_loop(0, ROWS // 16, body, 0, unroll=4)

    sent = []

    def number(name):
        return name if isinstance(name, int) else MESSAGES.index(name)

    def copy(m, src, dst, peer, r=None):
        return pltpu.make_async_remote_copy(
            src_ref=src, dst_ref=dst, send_sem=ssem.at[number(m)], recv_sem=rsem.at[number(m if r is None else r)],
            device_id=peer, device_id_type=MESH)

    def send(name, src, dst, peer, as_name=None, keep=True):
        c = copy(name, src, dst, peer, as_name)
        c.start()
        if keep:
            sent.append(c)

    def arrived(name, dst):
        copy(name, dst, dst, sib).wait_recv()

    a_half, b_half = pl.ds(0, H), pl.ds(H, H)
    OWN, LEFT, RIGHT, OPP = range(4)
    SIB, YP, YS = 1, 2, 3

    fetch[2].wait()
    PI[0] = jnp.broadcast_to(PIN[...], (8, LANES))
    fetch[0].wait()
    normalize(IM, Q.at[OWN], 0)
    pl.semaphore_wait(barrier, len(greeted))
    send("PIR", PI.at[OWN], PI.at[LEFT], right)
    send("PIL", PI.at[OWN], PI.at[RIGHT], left)
    send("PIO", PI.at[OWN], PI.at[OPP], opposite)
    send("QRa", Q.at[OWN, a_half], Q.at[LEFT, a_half], right)
    send("QLb", Q.at[OWN, b_half], Q.at[RIGHT, b_half], left)
    send("QRb", Q.at[OWN, b_half], Q.at[LEFT, b_half], right)
    send("QLa", Q.at[OWN, a_half], Q.at[RIGHT, a_half], left)
    fetch[1].wait()
    normalize(CAP, K.at[0, OWN], 1)
    send("KYa", K.at[0, OWN, a_half], K.at[0, YP, a_half], y_peer)

    @pl.when(last)
    def _():
        for i in range(H // 32):
            for lo, same, other in ((H, "KZb", "EB"), (0, "KZa", "FZ")):
                rows = pl.ds(lo + i * 32, 32)
                send(same, K.at[0, OWN, rows], K.at[1, OWN, rows], z_next, keep=False)
                send(other, K.at[0, OWN, rows], K.at[1, YP, rows], zy_next, "FY" if other == "EB" else None, keep=False)

    @pl.when(not_last)
    def _():
        send("KZb", K.at[0, OWN, b_half], K.at[1, OWN, b_half], z_next, keep=False)
        send("KZa", K.at[0, OWN, a_half], K.at[1, OWN, a_half], z_next, keep=False)

    send("KYb", K.at[0, OWN, b_half], K.at[0, YP, b_half], y_peer)
    send("KS", K.at[0, OWN], K.at[0, SIB], sib)

    own_base = [gat(yh, x, core), gat(yh, x, 1 - core), g_y, gat(1 - yh, x, 1 - core)]
    NT = (((1,), (1,)), ((), ()))
    TN = (((0,), (0,)), ((), ()))

    def fold(v):
        return (v[0:8] + v[8:16]) + (v[16:24] + v[24:32])

    def pair_terms(k, kp, s):
        keys = K[k, 2 * kp:2 * kp + 2].reshape(2 * ROWS, E)
        sims = lax.dot_general(keys, Q[s], NT, preferred_element_type=jnp.float32)
        cols = slice(s * ROWS, (s + 1) * ROWS)
        tot = None
        for i in range(8):
            ts = temper * sims[i * 32:(i + 1) * 32]
            logits = ts + bias
            p = jnp.exp(logits)
            d = 1.0 + p
            coeff = p / d
            prod = (d[0:8] * d[8:16]) * (d[16:24] * d[24:32])
            loss = jnp.log(prod)
            t = 2 * kp + i // 4
            if k == 0:
                cid = lax.broadcasted_iota(jnp.int32, (32, ROWS), 0) + (own_base[t] * ROWS + (i % 4) * 32)
                hit = cid == PI[s, 0:1]
                coeff = jnp.where(hit, coeff - 1.0, coeff)
                loss = loss - fold(jnp.where(hit, logits, 0.0))
            C[k, t, (i % 4) * 32:(i % 4) * 32 + 32, cols] = coeff.astype(jnp.bfloat16)
            new = (loss, fold(coeff * ts), fold(coeff))
            tot = new if tot is None else tuple(u + v for u, v in zip(tot, new))
        for j in range(3):
            SUMS[j] += tot[j]

    arrived("KS", K.at[0, SIB])
    pair_terms(0, 0, OWN)

    arrived("QRa", Q.at[LEFT, a_half])
    send("QFR", Q.at[LEFT, a_half], Q.at[OPP, a_half], right)
    arrived("QLb", Q.at[RIGHT, b_half])
    send("QFL", Q.at[RIGHT, b_half], Q.at[OPP, b_half], left)
    arrived("KYa", K.at[0, YP, a_half])

    @pl.when(not_last)
    def _():
        send("FZ", K.at[0, YP, a_half], K.at[1, YP, a_half], z_next, keep=False)

    send("S0a", K.at[0, YP, a_half], K.at[0, YS, a_half], sib)
    arrived("KZb", K.at[1, OWN, b_half])

    @pl.when(not_first)
    def _():
        send("FY", K.at[1, OWN, b_half], K.at[1, YP, b_half], y_peer, keep=False)

    send("S1b", K.at[1, OWN, b_half], K.at[1, SIB, b_half], sib)
    arrived("KYb", K.at[0, YP, b_half])
    send("S0b", K.at[0, YP, b_half], K.at[0, YS, b_half], sib)
    arrived("KZa", K.at[1, OWN, a_half])
    send("S1a", K.at[1, OWN, a_half], K.at[1, SIB, a_half], sib)
    arrived("QRb", Q.at[LEFT, b_half])
    arrived("QLa", Q.at[RIGHT, a_half])
    arrived("PIR", PI.at[LEFT])
    arrived("PIL", PI.at[RIGHT])
    pair_terms(0, 0, LEFT)
    pair_terms(0, 0, RIGHT)
    arrived("S0a", K.at[0, YS, a_half])
    arrived("S0b", K.at[0, YS, b_half])
    for s in (OWN, LEFT, RIGHT):
        pair_terms(0, 1, s)
    arrived("FZ", K.at[1, YP, a_half])
    send("S2a", K.at[1, YP, a_half], K.at[1, YS, a_half], sib)
    arrived("FY", K.at[1, YP, b_half])
    send("S2b", K.at[1, YP, b_half], K.at[1, YS, b_half], sib)
    arrived("S1b", K.at[1, SIB, b_half])
    arrived("S1a", K.at[1, SIB, a_half])
    for s in (OWN, LEFT, RIGHT):
        pair_terms(1, 0, s)
    arrived("PIO", PI.at[OPP])
    arrived("QFR", Q.at[OPP, a_half])
    arrived("QFL", Q.at[OPP, b_half])
    pair_terms(0, 0, OPP)
    pair_terms(0, 1, OPP)

    def key_part(k, slots):
        coeff = jnp.concatenate([C[k, t] for t in slots], axis=0)
        return jnp.dot(coeff, Q[...].reshape(4 * ROWS, E), preferred_element_type=jnp.float32)

    def swap(k):
        rows = pl.ds(ROWS, ROWS)
        SS[k] = key_part(k, (SIB, YS))
        send("G%dy" % k, SS.at[k, rows], RS.at[k, rows], sib)
        rows = pl.ds(0, ROWS)
        send("G%do" % k, SS.at[k, rows], RS.at[k, rows], sib)

    swap(0)
    pair_terms(1, 0, OPP)
    arrived("S2a", K.at[1, YS, a_half])
    arrived("S2b", K.at[1, YS, b_half])
    for s in (OWN, LEFT, RIGHT, OPP):
        pair_terms(1, 1, s)

    def image_part(slots):
        cols = slice(slots[0] * ROWS, (slots[-1] + 1) * ROWS)
        out = None
        for k in range(WINDOW):
            new = lax.dot_general(C[k, :, :, cols].reshape(4 * ROWS, -1), K[k].reshape(4 * ROWS, E), TN,
                                  preferred_element_type=jnp.float32)
            out = new if out is None else out + new
        for i, s in enumerate(slots):
            ACCQ[s] = out[i * ROWS:(i + 1) * ROWS]

    def code(name, terms):
        p = PARTS.index(name)

        def body(j, _):
            cs = pl.ds(pl.multiple_of(j * LANES, LANES), LANES)
            v = None
            for t in terms:
                if isinstance(t, str):
                    q = PARTS.index(t)
                    u = RP[q, :, cs].astype(jnp.int32).astype(jnp.float32) * RPS[q, :, cs]
                else:
                    u = t[0][t[1], cs]
                v = u if v is None else v + u
            m = jnp.max(jnp.abs(v), axis=0, keepdims=True)
            up = 32767.0 / jnp.maximum(m, 1e-30)
            SP[p, :, cs] = jnp.round(v * up).astype(jnp.int32).astype(jnp.int16)
            SPS[p, :, cs] = m * (1.0 / 32767.0)
            return 0
        lax.fori_loop(0, E // LANES, body, 0, unroll=3)

    def send_part(name, peer, to=None, keep=True):
        p = PARTS.index(name)
        q = p if to is None else PARTS.index(to)
        send(name, SP.at[p], RP.at[q], peer, to, keep)
        send(SCALES + p, SPS.at[p], RPS.at[q], peer, SCALES + q, keep)

    def part(name, terms, peer):
        code(name, terms)
        send_part(name, peer)

    def part_in(name):
        p = PARTS.index(name)
        arrived(name, RP.at[p])
        arrived(SCALES + p, RPS.at[p])

    swap(1)

    row = lax.broadcasted_iota(jnp.int32, (8, LANES), 0)
    mine = jnp.zeros((8, LANES), jnp.float32)
    for j in range(3):
        mine = jnp.where(row == j, jnp.sum(SUMS[j], axis=0, keepdims=True), mine)
    ST[0] = mine
    for i, peer in enumerate(stage1):
        send("T0%d" % i, ST.at[0], RT.at[0, i], peer)

    def stage_sum(st, peers):
        tot = ST[st]
        for i in range(len(peers)):
            arrived("T%d%d" % (st, i), RT.at[st, i])
            tot = tot + RT[st, i]
        return tot

    image_part((OPP,))
    part("XOa", [(ACCQ.at[OPP], a_half)], right)
    part("XOb", [(ACCQ.at[OPP], b_half)], left)
    ACCK[1] = key_part(1, (OWN, YP))
    arrived("G1y", RS.at[1, pl.ds(ROWS, ROWS)])
    own_a, own_b, y_a, y_b = pl.ds(0, H), pl.ds(H, H), pl.ds(2 * H, H), pl.ds(3 * H, H)
    code("Y1a", [(ACCK.at[1], y_a), (RS.at[1], y_a)])

    @pl.when(first)
    def _():
        send_part("Y1a", zy_prev, "DA", keep=False)

    @pl.when(last)
    def _():
        send_part("Y1a", z_prev, "Z1a", keep=False)

    @pl.when(inner)
    def _():
        send_part("Y1a", y_peer, keep=False)

    arrived("G1o", RS.at[1, pl.ds(0, ROWS)])
    zob = [(ACCK.at[1], own_b), (RS.at[1], own_b)]
    zoa = [(ACCK.at[1], own_a), (RS.at[1], own_a)]

    @pl.when(first)
    def _():
        code("Zob", zob)
        send_part("Zob", z_prev, keep=False)

    code("Z1b", [(ACCK.at[1], y_b), (RS.at[1], y_b)])

    @pl.when(first)
    def _():
        send_part("Z1b", zy_prev, "DB", keep=False)
        code("Zoa", zoa)
        send_part("Zoa", z_prev, keep=False)

    @pl.when(not_first)
    def _():
        send_part("Z1b", z_prev, keep=False)

    image_part((LEFT, RIGHT))
    part("XRb", [(ACCQ.at[RIGHT], b_half)], right)
    part("XLa", [(ACCQ.at[LEFT], a_half)], left)

    @pl.when(not_first)
    def _():
        code("Zob", zob)
        send_part("Zob", z_prev, keep=False)

    ACCK[0] = key_part(0, (OWN, YP))
    arrived("G0y", RS.at[0, pl.ds(ROWS, ROWS)])
    arrived("G0o", RS.at[0, pl.ds(0, ROWS)])
    y0a = [(ACCK.at[0], y_a), (RS.at[0], y_a)]

    @pl.when(not_before_last)
    def _():
        code("Y0a", y0a)
        send_part("Y0a", y_peer, keep=False)

    ST[1] = stage_sum(0, stage1)
    for i, peer in enumerate(stage2):
        send("T1%d" % i, ST.at[1], RT.at[1, i], peer)

    part_in("XOa")
    part("XRa", [(ACCQ.at[RIGHT], a_half), "XOa"], right)
    part_in("XOb")
    part("XLb", [(ACCQ.at[LEFT], b_half), "XOb"], left)
    @pl.when(last)
    def _():
        code("Zoa", zoa)
        send_part("Zoa", z_prev, keep=False)

    @pl.when(inner)
    def _():
        part_in("Y1a")
        code("Zoa", zoa + ["Y1a"])
        send_part("Zoa", z_prev, keep=False)

    y0b = [(ACCK.at[0], y_b), (RS.at[0], y_b)]

    @pl.when(before_last)
    def _():
        part_in("Z1a")
        code("Y0a", y0a + ["Z1a"])
        send_part("Y0a", y_peer, keep=False)

    @pl.when(last)
    def _():
        code("Y0b", y0b)

    @pl.when(not_last)
    def _():
        part_in("Z1b")
        code("Y0b", y0b + ["Z1b"])

    send_part("Y0b", y_peer)
    image_part((OWN,))

    ST[2] = stage_sum(1, stage2)
    for i, peer in enumerate(stage3):
        send("T2%d" % i, ST.at[2], RT.at[2, i], peer)

    def finish(half, src, which, own, parts, out):
        def body(i, _):
            local = pl.ds(pl.multiple_of(i * 16, 16), 16)
            rows = pl.ds(pl.multiple_of(half * H + i * 16, 16), 16)
            inv = INV[which, rows, 0:1]
            unit = src[rows, :].astype(jnp.float32) * inv
            grad = None
            for o in own:
                grad = o[rows, :] if grad is None else grad + o[rows, :]
            for name in parts:
                q = PARTS.index(name)
                grad = grad + RP[q, local, :].astype(jnp.int32).astype(jnp.float32) * RPS[q]
            grad = grad * temper[:, 0:1]
            along = jnp.sum(unit * grad, axis=1, keepdims=True)
            out[rows, :] = inv * (grad - unit * along)
            return 0
        lax.fori_loop(0, H // 16, body, 0, unroll=2)

    key_own = [ACCK.at[0], RS.at[0]]
    part_in("XRb")
    part_in("XLb")
    finish(1, IM, 0, [ACCQ.at[OWN]], ["XRb", "XLb"], GI)
    part_in("XRa")
    part_in("XLa")
    finish(0, IM, 0, [ACCQ.at[OWN]], ["XRa", "XLa"], GI)
    part_in("Zoa")
    part_in("Y0a")

    def finish_caption(half, names, extra):
        @pl.when(last)
        def _():
            part_in(extra)
            finish(half, CAP, 1, key_own, names + [extra], GC)

        @pl.when(not_last)
        def _():
            finish(half, CAP, 1, key_own, names, GC)


    finish_caption(0, ["Zoa", "Y0a"], "DA")
    part_in("Zob")
    part_in("Y0b")
    finish_caption(1, ["Zob", "Y0b"], "DB")

    tot = stage_sum(2, stage3)
    count = 1.0 / (n_blk * WINDOW * 2048.0 * 2048.0)
    for j, ref in ((0, loss_ref), (1, gs_ref), (2, gb_ref)):
        ref[0] = jnp.sum(tot[j:j + 1, :]) * count
    for c in sent:
        c.wait_send()
    copy("FZ", K.at[0, OWN, a_half], K.at[1, YP, a_half], sib).wait_send()
    copy("KZb", K.at[0, OWN, b_half], K.at[1, OWN, b_half], sib).wait_send()
    copy("KZa", K.at[0, OWN, a_half], K.at[1, OWN, a_half], sib).wait_send()
    for name in ("Y1a", "Z1b", "Y0a", "Zob", "Zoa"):
        p = PARTS.index(name)
        copy(name, SP.at[p], RP.at[p], sib).wait_send()
        copy(SCALES + p, SPS.at[p], RPS.at[p], sib).wait_send()

    @pl.when(last)
    def _():
        copy("EB", K.at[0, OWN, b_half], K.at[1, YP, b_half], zy_next, "FY").wait_send()

    @pl.when(not_first)
    def _():
        copy("FY", K.at[1, OWN, b_half], K.at[1, YP, b_half], y_peer).wait_send()


def on_device(n_blk, images, captions, pair_index, logit_scale, logit_bias):
    smem = pl.BlockSpec(memory_space=pltpu.SMEM)
    hbm = pl.BlockSpec(memory_space=pltpu.HBM)
    vmem = pl.BlockSpec(memory_space=pltpu.VMEM)
    f32, bf16, i16 = jnp.float32, jnp.bfloat16, jnp.int16
    one = jax.ShapeDtypeStruct((1,), f32)
    grad = jax.ShapeDtypeStruct((ROWS, E), f32)
    unit = (ROWS, E)
    n = len(PARTS)
    return pl.pallas_call(
        functools.partial(kernel, n_blk),
        out_shape=(one, grad, grad, one, one),
        in_specs=[hbm, hbm, hbm, smem, smem],
        out_specs=(smem, vmem, vmem, smem, smem),
        scratch_shapes=[
            pltpu.VMEM(unit, bf16),
            pltpu.VMEM(unit, bf16),
            pltpu.VMEM((1, LANES), jnp.int32),
            pltpu.VMEM((4,) + unit, bf16),
            pltpu.VMEM((4, 8, LANES), jnp.int32),
            pltpu.VMEM((2, 4) + unit, bf16),
            pltpu.VMEM((2, 4, ROWS, 4 * ROWS), bf16),
            pltpu.VMEM((2, ROWS, LANES), f32),
            pltpu.VMEM((4,) + unit, f32),
            pltpu.VMEM((2, 2 * ROWS, E), f32),
            pltpu.VMEM((2, 2 * ROWS, E), f32),
            pltpu.VMEM((2, 2 * ROWS, E), f32),
            pltpu.VMEM((n, H, E), i16),
            pltpu.VMEM((n, 1, E), f32),
            pltpu.VMEM((n, H, E), i16),
            pltpu.VMEM((n, 1, E), f32),
            pltpu.VMEM((3, 8, LANES), f32),
            pltpu.VMEM((3, 7, 8, LANES), f32),
            pltpu.VMEM((3, 8, LANES), f32),
            pltpu.SemaphoreType.DMA((3,)),
            pltpu.SemaphoreType.DMA((N_MSG,)),
            pltpu.SemaphoreType.DMA((N_MSG,)),
        ],
        compiler_params=pltpu.CompilerParams(
            collective_id=0, has_side_effects=True, vmem_limit_bytes=60 * 2**20),
    )(images, captions, pair_index, logit_scale, logit_bias)


def solution(mesh):
    placed = (P(("blk", "gather"), None), P(("blk", "gather"), None), P("blk", "gather"), P(), P())
    return jax.shard_map(
        functools.partial(on_device, mesh.shape["blk"]),
        mesh=mesh,
        in_specs=placed,
        out_specs=(P(), P(("blk", "gather"), None), P(("blk", "gather"), None), P(), P()),
        check_vma=False,
    )
```

```python
import functools

import jax
import jax.numpy as jnp
from jax import lax
from jax.experimental import pallas as pl
from jax.experimental.pallas import tpu as pltpu
from jax.sharding import PartitionSpec as P

MESH = pl.DeviceIdType.MESH
EPS = 1e-06
WINDOW = 2
NX = 4
ROWS = 128
E = 1152
LANES = 128

H = ROWS // 2

MESSAGES = [
    "QRa", "QRb", "QLb", "QLa", "QFR", "QFL", "PIR", "PIL", "PIO",
    "KYa", "KYb", "KZa", "KZb", "KS", "FZ", "FY", "S0a", "S0b", "S1a", "S1b", "S2a", "S2b",
    "XOa", "XOb", "XRa", "XRb", "XLa", "XLb", "Y1a", "Y0a", "Y0b", "Z1b", "Zob", "Zoa",
    "G1y", "G1o", "G0y", "G0o", "DA", "DB", "Z1a", "EB",
] + ["T%d%d" % (i, j) for i in range(3) for j in range(7)]
PARTS = ["XOa", "XOb", "XRa", "XRb", "XLa", "XLb", "Y1a", "Y0a", "Y0b", "Z1b", "Zob", "Zoa", "DA", "DB", "Z1a"]
SCALES = len(MESSAGES)
N_MSG = SCALES + len(PARTS)


def kernel(n_blk, im_hbm, cap_hbm, pi_hbm, ls_ref, lb_ref,
           loss_ref, GI, GC, gs_ref, gb_ref,
           IM, CAP, PIN, Q, PI, K, C, INV, ACCQ, ACCK, SS, RS,
           SP, SPS, RP, RPS, ST, RT, SUMS, isem, ssem, rsem):
    b = lax.axis_index("blk")
    g = lax.axis_index("gather")
    core = lax.rem(g, 2)
    x = lax.rem(g // 2, NX)
    yh = g // (2 * NX)
    nz = n_blk // 2
    zl_n = min(4, nz)
    zh_n = nz // zl_n
    z = lax.rem(b, nz)
    yl = b // nz
    zl = lax.rem(z, zl_n)
    zh = z // zl_n

    def gat(yh_, x_, core_):
        return yh_ * (2 * NX) + lax.rem(x_, NX) * 2 + core_

    def blk(yl_, zh_, zl_):
        return yl_ * nz + zh_ * zl_n + zl_

    g_y = gat(1 - yh, x, core)
    right = (b, gat(yh, x + 1, core))
    left = (b, gat(yh, x + 3, core))
    opposite = (b, gat(yh, x + 2, core))
    b_n = lax.rem(b + 1, n_blk)
    b_p = lax.rem(b + n_blk - 1, n_blk)
    sib = (b, gat(yh, x, 1 - core))
    y_peer = (b, g_y)
    z_next = (b_n, g)
    z_prev = (b_p, g)
    first, last = z == 0, z == nz - 1
    not_first, not_last = z != 0, z != nz - 1
    inner = jnp.logical_and(not_first, not_last)
    before_last, not_before_last = z == nz - 2, z != nz - 2
    zy_next = (b_n, g_y)
    zy_prev = (b_p, g_y)
    stage1 = []
    for i in range(1, 8):
        j = lax.rem(lax.rem(g, 8) + i, 8)
        stage1.append((b, yh * 8 + j))
    n2, n3 = 2 * zl_n, 2 * zh_n
    stage2 = []
    for i in range(1, n2):
        j = lax.rem(yh * zl_n + zl + i, n2)
        stage2.append((blk(yl, zh, lax.rem(j, zl_n)), gat(j // zl_n, x, core)))
    stage3 = []
    for i in range(1, n3):
        j = lax.rem(yl * zh_n + zh + i, n3)
        stage3.append((blk(j // zh_n, lax.rem(j, zh_n), zl), g))

    barrier = pltpu.get_barrier_semaphore()
    greeted = stage1 + stage2 + stage3 + [z_next, z_prev, zy_next, zy_prev]
    for peer in greeted:
        pl.semaphore_signal(barrier, inc=1, device_id=peer, device_id_type=MESH)

    fetch = [pltpu.make_async_copy(im_hbm, IM, isem.at[0]), pltpu.make_async_copy(cap_hbm, CAP, isem.at[1]),
             pltpu.make_async_copy(pi_hbm, PIN, isem.at[2])]
    for f in fetch:
        f.start()

    temper = jnp.exp(jnp.full((1, LANES), ls_ref[0], jnp.float32))
    bias = lb_ref[0]
    SUMS[...] = jnp.zeros_like(SUMS)

    def normalize(src, dst, which):
        def body(i, _):
            rows = pl.ds(pl.multiple_of(i * 16, 16), 16)
            v = src[rows, :].astype(jnp.float32)
            inv = lax.rsqrt(jnp.sum(v * v, axis=1, keepdims=True) + EPS)
            INV[which, rows, :] = jnp.broadcast_to(inv, (16, LANES))
            dst[rows, :] = (v * inv).astype(jnp.bfloat16)
            return 0
        lax.fori_loop(0, ROWS // 16, body, 0, unroll=4)

    sent = []

    def number(name):
        return name if isinstance(name, int) else MESSAGES.index(name)

    def copy(m, src, dst, peer, r=None):
        return pltpu.make_async_remote_copy(
            src_ref=src, dst_ref=dst, send_sem=ssem.at[number(m)], recv_sem=rsem.at[number(m if r is None else r)],
            device_id=peer, device_id_type=MESH)

    def send(name, src, dst, peer, as_name=None, keep=True):
        c = copy(name, src, dst, peer, as_name)
        c.start()
        if keep:
            sent.append(c)

    def arrived(name, dst):
        copy(name, dst, dst, sib).wait_recv()

    a_half, b_half = pl.ds(0, H), pl.ds(H, H)
    OWN, LEFT, RIGHT, OPP = range(4)
    SIB, YP, YS = 1, 2, 3

    fetch[2].wait()
    PI[0] = jnp.broadcast_to(PIN[...], (8, LANES))
    fetch[1].wait()
    normalize(CAP, K.at[0, OWN], 1)
    pl.semaphore_wait(barrier, len(greeted))
    send("KYa", K.at[0, OWN, a_half], K.at[0, YP, a_half], y_peer)

    @pl.when(last)
    def _():
        for i in range(H // 32):
            for lo, same, other in ((H, "KZb", "EB"), (0, "KZa", "FZ")):
                rows = pl.ds(lo + i * 32, 32)
                send(same, K.at[0, OWN, rows], K.at[1, OWN, rows], z_next, keep=False)
                send(other, K.at[0, OWN, rows], K.at[1, YP, rows], zy_next, "FY" if other == "EB" else None, keep=False)

    @pl.when(not_last)
    def _():
        send("KZb", K.at[0, OWN, b_half], K.at[1, OWN, b_half], z_next, keep=False)
        send("KZa", K.at[0, OWN, a_half], K.at[1, OWN, a_half], z_next, keep=False)

    send("KYb", K.at[0, OWN, b_half], K.at[0, YP, b_half], y_peer)
    send("KS", K.at[0, OWN], K.at[0, SIB], sib)

    fetch[0].wait()
    normalize(IM, Q.at[OWN], 0)
    send("PIR", PI.at[OWN], PI.at[LEFT], right)
    send("PIL", PI.at[OWN], PI.at[RIGHT], left)
    send("PIO", PI.at[OWN], PI.at[OPP], opposite)
    send("QRa", Q.at[OWN, a_half], Q.at[LEFT, a_half], right)
    send("QLb", Q.at[OWN, b_half], Q.at[RIGHT, b_half], left)
    send("QRb", Q.at[OWN, b_half], Q.at[LEFT, b_half], right)
    send("QLa", Q.at[OWN, a_half], Q.at[RIGHT, a_half], left)

    own_base = [gat(yh, x, core), gat(yh, x, 1 - core), g_y, gat(1 - yh, x, 1 - core)]
    NT = (((1,), (1,)), ((), ()))
    TN = (((0,), (0,)), ((), ()))

    def fold(v):
        return (v[0:8] + v[8:16]) + (v[16:24] + v[24:32])

    def pair_terms(k, kp, s):
        keys = K[k, 2 * kp:2 * kp + 2].reshape(2 * ROWS, E)
        sims = lax.dot_general(keys, Q[s], NT, preferred_element_type=jnp.float32)
        cols = slice(s * ROWS, (s + 1) * ROWS)
        tot = None
        for i in range(8):
            ts = temper * sims[i * 32:(i + 1) * 32]
            logits = ts + bias
            p = jnp.exp(logits)
            d = 1.0 + p
            coeff = p / d
            prod = (d[0:8] * d[8:16]) * (d[16:24] * d[24:32])
            loss = jnp.log(prod)
            t = 2 * kp + i // 4
            if k == 0:
                cid = lax.broadcasted_iota(jnp.int32, (32, ROWS), 0) + (own_base[t] * ROWS + (i % 4) * 32)
                hit = cid == PI[s, 0:1]
                coeff = jnp.where(hit, coeff - 1.0, coeff)
                loss = loss - fold(jnp.where(hit, logits, 0.0))
            C[k, t, (i % 4) * 32:(i % 4) * 32 + 32, cols] = coeff.astype(jnp.bfloat16)
            new = (loss, fold(coeff * ts), fold(coeff))
            tot = new if tot is None else tuple(u + v for u, v in zip(tot, new))
        for j in range(3):
            SUMS[j] += tot[j]

    arrived("KS", K.at[0, SIB])
    pair_terms(0, 0, OWN)

    arrived("QRa", Q.at[LEFT, a_half])
    send("QFR", Q.at[LEFT, a_half], Q.at[OPP, a_half], right)
    arrived("QLb", Q.at[RIGHT, b_half])
    send("QFL", Q.at[RIGHT, b_half], Q.at[OPP, b_half], left)
    arrived("KYa", K.at[0, YP, a_half])

    @pl.when(not_last)
    def _():
        send("FZ", K.at[0, YP, a_half], K.at[1, YP, a_half], z_next, keep=False)

    send("S0a", K.at[0, YP, a_half], K.at[0, YS, a_half], sib)
    arrived("KZb", K.at[1, OWN, b_half])

    @pl.when(not_first)
    def _():
        send("FY", K.at[1, OWN, b_half], K.at[1, YP, b_half], y_peer, keep=False)

    send("S1b", K.at[1, OWN, b_half], K.at[1, SIB, b_half], sib)
    arrived("KYb", K.at[0, YP, b_half])
    send("S0b", K.at[0, YP, b_half], K.at[0, YS, b_half], sib)
    arrived("KZa", K.at[1, OWN, a_half])
    send("S1a", K.at[1, OWN, a_half], K.at[1, SIB, a_half], sib)
    arrived("QRb", Q.at[LEFT, b_half])
    arrived("QLa", Q.at[RIGHT, a_half])
    arrived("PIR", PI.at[LEFT])
    arrived("PIL", PI.at[RIGHT])
    pair_terms(0, 0, LEFT)
    pair_terms(0, 0, RIGHT)
    arrived("S0a", K.at[0, YS, a_half])
    arrived("S0b", K.at[0, YS, b_half])
    for s in (OWN, LEFT, RIGHT):
        pair_terms(0, 1, s)
    arrived("FZ", K.at[1, YP, a_half])
    send("S2a", K.at[1, YP, a_half], K.at[1, YS, a_half], sib)
    arrived("FY", K.at[1, YP, b_half])
    send("S2b", K.at[1, YP, b_half], K.at[1, YS, b_half], sib)
    arrived("S1b", K.at[1, SIB, b_half])
    arrived("S1a", K.at[1, SIB, a_half])
    for s in (OWN, LEFT, RIGHT):
        pair_terms(1, 0, s)
    arrived("PIO", PI.at[OPP])
    arrived("QFR", Q.at[OPP, a_half])
    arrived("QFL", Q.at[OPP, b_half])
    pair_terms(0, 0, OPP)
    pair_terms(0, 1, OPP)

    def key_part(k, slots):
        coeff = jnp.concatenate([C[k, t] for t in slots], axis=0)
        return jnp.dot(coeff, Q[...].reshape(4 * ROWS, E), preferred_element_type=jnp.float32)

    def swap(k):
        rows = pl.ds(ROWS, ROWS)
        SS[k] = key_part(k, (SIB, YS))
        send("G%dy" % k, SS.at[k, rows], RS.at[k, rows], sib)
        rows = pl.ds(0, ROWS)
        send("G%do" % k, SS.at[k, rows], RS.at[k, rows], sib)

    swap(0)
    pair_terms(1, 0, OPP)
    arrived("S2a", K.at[1, YS, a_half])
    arrived("S2b", K.at[1, YS, b_half])
    for s in (OWN, LEFT, RIGHT, OPP):
        pair_terms(1, 1, s)

    def image_part(slots):
        cols = slice(slots[0] * ROWS, (slots[-1] + 1) * ROWS)
        out = None
        for k in range(WINDOW):
            new = lax.dot_general(C[k, :, :, cols].reshape(4 * ROWS, -1), K[k].reshape(4 * ROWS, E), TN,
                                  preferred_element_type=jnp.float32)
            out = new if out is None else out + new
        for i, s in enumerate(slots):
            ACCQ[s] = out[i * ROWS:(i + 1) * ROWS]

    def code(name, terms):
        p = PARTS.index(name)

        def body(j, _):
            cs = pl.ds(pl.multiple_of(j * LANES, LANES), LANES)
            v = None
            for t in terms:
                if isinstance(t, str):
                    q = PARTS.index(t)
                    u = RP[q, :, cs].astype(jnp.int32).astype(jnp.float32) * RPS[q, :, cs]
                else:
                    u = t[0][t[1], cs]
                v = u if v is None else v + u
            m = jnp.max(jnp.abs(v), axis=0, keepdims=True)
            up = 32767.0 / jnp.maximum(m, 1e-30)
            SP[p, :, cs] = jnp.round(v * up).astype(jnp.int32).astype(jnp.int16)
            SPS[p, :, cs] = m * (1.0 / 32767.0)
            return 0
        lax.fori_loop(0, E // LANES, body, 0, unroll=3)

    def send_part(name, peer, to=None, keep=True):
        p = PARTS.index(name)
        q = p if to is None else PARTS.index(to)
        send(name, SP.at[p], RP.at[q], peer, to, keep)
        send(SCALES + p, SPS.at[p], RPS.at[q], peer, SCALES + q, keep)

    def part(name, terms, peer):
        code(name, terms)
        send_part(name, peer)

    def part_in(name):
        p = PARTS.index(name)
        arrived(name, RP.at[p])
        arrived(SCALES + p, RPS.at[p])

    swap(1)

    row = lax.broadcasted_iota(jnp.int32, (8, LANES), 0)
    mine = jnp.zeros((8, LANES), jnp.float32)
    for j in range(3):
        mine = jnp.where(row == j, jnp.sum(SUMS[j], axis=0, keepdims=True), mine)
    ST[0] = mine
    for i, peer in enumerate(stage1):
        send("T0%d" % i, ST.at[0], RT.at[0, i], peer)

    def stage_sum(st, peers):
        tot = ST[st]
        for i in range(len(peers)):
            arrived("T%d%d" % (st, i), RT.at[st, i])
            tot = tot + RT[st, i]
        return tot

    image_part((OPP,))
    part("XOa", [(ACCQ.at[OPP], a_half)], right)
    part("XOb", [(ACCQ.at[OPP], b_half)], left)
    ACCK[1] = key_part(1, (OWN, YP))
    arrived("G1y", RS.at[1, pl.ds(ROWS, ROWS)])
    own_a, own_b, y_a, y_b = pl.ds(0, H), pl.ds(H, H), pl.ds(2 * H, H), pl.ds(3 * H, H)
    code("Y1a", [(ACCK.at[1], y_a), (RS.at[1], y_a)])

    @pl.when(first)
    def _():
        send_part("Y1a", zy_prev, "DA", keep=False)

    @pl.when(last)
    def _():
        send_part("Y1a", z_prev, "Z1a", keep=False)

    @pl.when(inner)
    def _():
        send_part("Y1a", y_peer, keep=False)

    arrived("G1o", RS.at[1, pl.ds(0, ROWS)])
    zob = [(ACCK.at[1], own_b), (RS.at[1], own_b)]
    zoa = [(ACCK.at[1], own_a), (RS.at[1], own_a)]

    @pl.when(first)
    def _():
        code("Zob", zob)
        send_part("Zob", z_prev, keep=False)

    code("Z1b", [(ACCK.at[1], y_b), (RS.at[1], y_b)])

    @pl.when(first)
    def _():
        send_part("Z1b", zy_prev, "DB", keep=False)
        code("Zoa", zoa)
        send_part("Zoa", z_prev, keep=False)

    @pl.when(not_first)
    def _():
        send_part("Z1b", z_prev, keep=False)

    image_part((LEFT, RIGHT))
    part("XRb", [(ACCQ.at[RIGHT], b_half)], right)
    part("XLa", [(ACCQ.at[LEFT], a_half)], left)

    @pl.when(not_first)
    def _():
        code("Zob", zob)
        send_part("Zob", z_prev, keep=False)

    ACCK[0] = key_part(0, (OWN, YP))
    arrived("G0y", RS.at[0, pl.ds(ROWS, ROWS)])
    arrived("G0o", RS.at[0, pl.ds(0, ROWS)])
    y0a = [(ACCK.at[0], y_a), (RS.at[0], y_a)]

    @pl.when(not_before_last)
    def _():
        code("Y0a", y0a)
        send_part("Y0a", y_peer, keep=False)

    ST[1] = stage_sum(0, stage1)
    for i, peer in enumerate(stage2):
        send("T1%d" % i, ST.at[1], RT.at[1, i], peer)

    part_in("XOa")
    part("XRa", [(ACCQ.at[RIGHT], a_half), "XOa"], right)
    part_in("XOb")
    part("XLb", [(ACCQ.at[LEFT], b_half), "XOb"], left)
    @pl.when(last)
    def _():
        code("Zoa", zoa)
        send_part("Zoa", z_prev, keep=False)

    @pl.when(inner)
    def _():
        part_in("Y1a")
        code("Zoa", zoa + ["Y1a"])
        send_part("Zoa", z_prev, keep=False)

    y0b = [(ACCK.at[0], y_b), (RS.at[0], y_b)]

    @pl.when(before_last)
    def _():
        part_in("Z1a")
        code("Y0a", y0a + ["Z1a"])
        send_part("Y0a", y_peer, keep=False)

    @pl.when(last)
    def _():
        code("Y0b", y0b)

    @pl.when(not_last)
    def _():
        part_in("Z1b")
        code("Y0b", y0b + ["Z1b"])

    send_part("Y0b", y_peer)
    image_part((OWN,))

    ST[2] = stage_sum(1, stage2)
    for i, peer in enumerate(stage3):
        send("T2%d" % i, ST.at[2], RT.at[2, i], peer)

    def finish(half, src, which, own, parts, out):
        def body(i, _):
            local = pl.ds(pl.multiple_of(i * 16, 16), 16)
            rows = pl.ds(pl.multiple_of(half * H + i * 16, 16), 16)
            inv = INV[which, rows, 0:1]
            unit = src[rows, :].astype(jnp.float32) * inv
            grad = None
            for o in own:
                grad = o[rows, :] if grad is None else grad + o[rows, :]
            for name in parts:
                q = PARTS.index(name)
                grad = grad + RP[q, local, :].astype(jnp.int32).astype(jnp.float32) * RPS[q]
            along = jnp.sum(unit * grad, axis=1, keepdims=True)
            out[rows, :] = inv * (grad - unit * along)
            return 0
        lax.fori_loop(0, H // 16, body, 0, unroll=2)

    key_own = [ACCK.at[0], RS.at[0]]
    part_in("XRb")
    part_in("XLb")
    finish(1, IM, 0, [ACCQ.at[OWN]], ["XRb", "XLb"], GI)
    part_in("XRa")
    part_in("XLa")
    finish(0, IM, 0, [ACCQ.at[OWN]], ["XRa", "XLa"], GI)
    part_in("Zoa")
    part_in("Y0a")

    def finish_caption(half, names, extra):
        @pl.when(last)
        def _():
            part_in(extra)
            finish(half, CAP, 1, key_own, names + [extra], GC)

        @pl.when(not_last)
        def _():
            finish(half, CAP, 1, key_own, names, GC)


    finish_caption(0, ["Zoa", "Y0a"], "DA")
    part_in("Zob")
    part_in("Y0b")
    finish_caption(1, ["Zob", "Y0b"], "DB")

    tot = stage_sum(2, stage3)
    count = 1.0 / (n_blk * WINDOW * 2048.0 * 2048.0)
    for j, ref in ((0, loss_ref), (1, gs_ref), (2, gb_ref)):
        ref[0] = jnp.sum(tot[j:j + 1, :]) * count
    for c in sent:
        c.wait_send()
    copy("FZ", K.at[0, OWN, a_half], K.at[1, YP, a_half], sib).wait_send()
    copy("KZb", K.at[0, OWN, b_half], K.at[1, OWN, b_half], sib).wait_send()
    copy("KZa", K.at[0, OWN, a_half], K.at[1, OWN, a_half], sib).wait_send()
    for name in ("Y1a", "Z1b", "Y0a", "Zob", "Zoa"):
        p = PARTS.index(name)
        copy(name, SP.at[p], RP.at[p], sib).wait_send()
        copy(SCALES + p, SPS.at[p], RPS.at[p], sib).wait_send()

    @pl.when(last)
    def _():
        copy("EB", K.at[0, OWN, b_half], K.at[1, YP, b_half], zy_next, "FY").wait_send()

    @pl.when(not_first)
    def _():
        copy("FY", K.at[1, OWN, b_half], K.at[1, YP, b_half], y_peer).wait_send()


def on_device(n_blk, images, captions, pair_index, logit_scale, logit_bias):
    smem = pl.BlockSpec(memory_space=pltpu.SMEM)
    hbm = pl.BlockSpec(memory_space=pltpu.HBM)
    vmem = pl.BlockSpec(memory_space=pltpu.VMEM)
    f32, bf16, i16 = jnp.float32, jnp.bfloat16, jnp.int16
    one = jax.ShapeDtypeStruct((1,), f32)
    grad = jax.ShapeDtypeStruct((ROWS, E), f32)
    unit = (ROWS, E)
    n = len(PARTS)
    loss, grad_images, grad_captions, grad_scale, grad_bias = pl.pallas_call(
        functools.partial(kernel, n_blk),
        out_shape=(one, grad, grad, one, one),
        in_specs=[hbm, hbm, hbm, smem, smem],
        out_specs=(smem, vmem, vmem, smem, smem),
        scratch_shapes=[
            pltpu.VMEM(unit, bf16),
            pltpu.VMEM(unit, bf16),
            pltpu.VMEM((1, LANES), jnp.int32),
            pltpu.VMEM((4,) + unit, bf16),
            pltpu.VMEM((4, 8, LANES), jnp.int32),
            pltpu.VMEM((2, 4) + unit, bf16),
            pltpu.VMEM((2, 4, ROWS, 4 * ROWS), bf16),
            pltpu.VMEM((2, ROWS, LANES), f32),
            pltpu.VMEM((4,) + unit, f32),
            pltpu.VMEM((2, 2 * ROWS, E), f32),
            pltpu.VMEM((2, 2 * ROWS, E), f32),
            pltpu.VMEM((2, 2 * ROWS, E), f32),
            pltpu.VMEM((n, H, E), i16),
            pltpu.VMEM((n, 1, E), f32),
            pltpu.VMEM((n, H, E), i16),
            pltpu.VMEM((n, 1, E), f32),
            pltpu.VMEM((3, 8, LANES), f32),
            pltpu.VMEM((3, 7, 8, LANES), f32),
            pltpu.VMEM((3, 8, LANES), f32),
            pltpu.SemaphoreType.DMA((3,)),
            pltpu.SemaphoreType.DMA((N_MSG,)),
            pltpu.SemaphoreType.DMA((N_MSG,)),
        ],
        compiler_params=pltpu.CompilerParams(
            collective_id=0, has_side_effects=True, vmem_limit_bytes=60 * 2**20),
    )(images, captions, pair_index, logit_scale, logit_bias)
    temper = jnp.exp(logit_scale[0])
    return loss, temper * grad_images, temper * grad_captions, grad_scale, grad_bias


def solution(mesh):
    placed = (P(("blk", "gather"), None), P(("blk", "gather"), None), P("blk", "gather"), P(), P())
    return jax.shard_map(
        functools.partial(on_device, mesh.shape["blk"]),
        mesh=mesh,
        in_specs=placed,
        out_specs=(P(), P(("blk", "gather"), None), P(("blk", "gather"), None), P(), P()),
        check_vma=False,
    )
```

```python
import functools

import jax
import jax.numpy as jnp
from jax import lax
from jax.experimental import pallas as pl
from jax.experimental.pallas import tpu as pltpu
from jax.sharding import PartitionSpec as P

MESH = pl.DeviceIdType.MESH
EPS = 1e-06
WINDOW = 2
NX = 4
ROWS = 128
E = 1152
LANES = 128

H = ROWS // 2

MESSAGES = [
    "QRa", "QRb", "QLb", "QLa", "QFR", "QFL", "PIR", "PIL", "PIO",
    "KYa", "KYb", "KZa", "KZb", "KS", "FZ", "FY", "S0a", "S0b", "S1a", "S1b", "S2a", "S2b",
    "XOa", "XOb", "XRa", "XRb", "XLa", "XLb", "Y1a", "Y0a", "Y0b", "Z1b", "Zob", "Zoa",
    "G1y", "G1o", "G0y", "G0o", "DA", "DB", "Z1a", "EB",
] + ["T%d%d" % (i, j) for i in range(3) for j in range(7)]
PARTS = ["XOa", "XOb", "XRa", "XRb", "XLa", "XLb", "Y1a", "Y0a", "Y0b", "Z1b", "Zob", "Zoa", "DA", "DB", "Z1a"]
SCALES = len(MESSAGES)
N_MSG = SCALES + len(PARTS)


def kernel(n_blk, im_hbm, cap_hbm, pi_hbm, ls_ref, lb_ref,
           loss_ref, GI, GC, gs_ref, gb_ref,
           IM, CAP, PIN, Q, PI, K, C, INV, ACCQ, ACCK, SS, RS,
           SP, SPS, RP, RPS, ST, RT, SUMS, isem, ssem, rsem):
    b = lax.axis_index("blk")
    g = lax.axis_index("gather")
    core = lax.rem(g, 2)
    x = lax.rem(g // 2, NX)
    yh = g // (2 * NX)
    nz = n_blk // 2
    zl_n = min(4, nz)
    zh_n = nz // zl_n
    z = lax.rem(b, nz)
    yl = b // nz
    zl = lax.rem(z, zl_n)
    zh = z // zl_n

    def gat(yh_, x_, core_):
        return yh_ * (2 * NX) + lax.rem(x_, NX) * 2 + core_

    def blk(yl_, zh_, zl_):
        return yl_ * nz + zh_ * zl_n + zl_

    g_y = gat(1 - yh, x, core)
    right = (b, gat(yh, x + 1, core))
    left = (b, gat(yh, x + 3, core))
    opposite = (b, gat(yh, x + 2, core))
    b_n = lax.rem(b + 1, n_blk)
    b_p = lax.rem(b + n_blk - 1, n_blk)
    sib = (b, gat(yh, x, 1 - core))
    y_peer = (b, g_y)
    z_next = (b_n, g)
    z_prev = (b_p, g)
    first, last = z == 0, z == nz - 1
    not_first, not_last = z != 0, z != nz - 1
    inner = jnp.logical_and(not_first, not_last)
    before_last, not_before_last = z == nz - 2, z != nz - 2
    zy_next = (b_n, g_y)
    zy_prev = (b_p, g_y)
    stage1 = []
    for i in range(1, 8):
        j = lax.rem(lax.rem(g, 8) + i, 8)
        stage1.append((b, yh * 8 + j))
    n2, n3 = 2 * zl_n, 2 * zh_n
    stage2 = []
    for i in range(1, n2):
        j = lax.rem(yh * zl_n + zl + i, n2)
        stage2.append((blk(yl, zh, lax.rem(j, zl_n)), gat(j // zl_n, x, core)))
    stage3 = []
    for i in range(1, n3):
        j = lax.rem(yl * zh_n + zh + i, n3)
        stage3.append((blk(j // zh_n, lax.rem(j, zh_n), zl), g))

    barrier = pltpu.get_barrier_semaphore()
    greeted = stage1 + stage2 + stage3 + [z_next, z_prev, zy_next, zy_prev]
    for peer in greeted:
        pl.semaphore_signal(barrier, inc=1, device_id=peer, device_id_type=MESH)

    fetch = [pltpu.make_async_copy(im_hbm, IM, isem.at[0]), pltpu.make_async_copy(cap_hbm, CAP, isem.at[1]),
             pltpu.make_async_copy(pi_hbm, PIN, isem.at[2])]
    for f in fetch:
        f.start()

    temper = jnp.exp(jnp.full((1, LANES), ls_ref[0], jnp.float32))
    bias = lb_ref[0]
    SUMS[...] = jnp.zeros_like(SUMS)

    def normalize(src, dst, which):
        def body(i, _):
            rows = pl.ds(pl.multiple_of(i * 16, 16), 16)
            v = src[rows, :].astype(jnp.float32)
            inv = lax.rsqrt(jnp.sum(v * v, axis=1, keepdims=True) + EPS)
            INV[which, rows, :] = jnp.broadcast_to(inv, (16, LANES))
            dst[rows, :] = (v * inv).astype(jnp.bfloat16)
            return 0
        lax.fori_loop(0, ROWS // 16, body, 0, unroll=4)

    sent = []

    def number(name):
        return name if isinstance(name, int) else MESSAGES.index(name)

    def copy(m, src, dst, peer, r=None):
        return pltpu.make_async_remote_copy(
            src_ref=src, dst_ref=dst, send_sem=ssem.at[number(m)], recv_sem=rsem.at[number(m if r is None else r)],
            device_id=peer, device_id_type=MESH)

    def send(name, src, dst, peer, as_name=None, keep=True):
        c = copy(name, src, dst, peer, as_name)
        c.start()
        if keep:
            sent.append(c)

    def arrived(name, dst):
        copy(name, dst, dst, sib).wait_recv()

    a_half, b_half = pl.ds(0, H), pl.ds(H, H)
    OWN, LEFT, RIGHT, OPP = range(4)
    SIB, YP, YS = 1, 2, 3

    fetch[2].wait()
    PI[0] = jnp.broadcast_to(PIN[...], (8, LANES))
    fetch[1].wait()
    normalize(CAP, K.at[0, OWN], 1)
    pl.semaphore_wait(barrier, len(greeted))
    send("KYa", K.at[0, OWN, a_half], K.at[0, YP, a_half], y_peer)

    @pl.when(last)
    def _():
        for i in range(H // 32):
            for lo, same, other in ((H, "KZb", "EB"), (0, "KZa", "FZ")):
                rows = pl.ds(lo + i * 32, 32)
                send(same, K.at[0, OWN, rows], K.at[1, OWN, rows], z_next, keep=False)
                send(other, K.at[0, OWN, rows], K.at[1, YP, rows], zy_next, "FY" if other == "EB" else None, keep=False)

    @pl.when(not_last)
    def _():
        send("KZb", K.at[0, OWN, b_half], K.at[1, OWN, b_half], z_next, keep=False)
        send("KZa", K.at[0, OWN, a_half], K.at[1, OWN, a_half], z_next, keep=False)

    send("KYb", K.at[0, OWN, b_half], K.at[0, YP, b_half], y_peer)
    send("KS", K.at[0, OWN], K.at[0, SIB], sib)

    fetch[0].wait()
    normalize(IM, Q.at[OWN], 0)
    send("PIR", PI.at[OWN], PI.at[LEFT], right)
    send("PIL", PI.at[OWN], PI.at[RIGHT], left)
    send("PIO", PI.at[OWN], PI.at[OPP], opposite)
    send("QRa", Q.at[OWN, a_half], Q.at[LEFT, a_half], right)
    send("QLb", Q.at[OWN, b_half], Q.at[RIGHT, b_half], left)
    send("QRb", Q.at[OWN, b_half], Q.at[LEFT, b_half], right)
    send("QLa", Q.at[OWN, a_half], Q.at[RIGHT, a_half], left)

    own_base = [gat(yh, x, core), gat(yh, x, 1 - core), g_y, gat(1 - yh, x, 1 - core)]
    NT = (((1,), (1,)), ((), ()))
    TN = (((0,), (0,)), ((), ()))

    def fold(v):
        return (v[0:8] + v[8:16]) + (v[16:24] + v[24:32])

    def pair_terms(k, kp, s):
        keys = K[k, 2 * kp:2 * kp + 2].reshape(2 * ROWS, E)
        sims = lax.dot_general(keys, Q[s], NT, preferred_element_type=jnp.float32)
        cols = slice(s * ROWS, (s + 1) * ROWS)
        tot = None
        for i in range(8):
            ts = temper * sims[i * 32:(i + 1) * 32]
            logits = ts + bias
            p = jnp.exp(logits)
            d = 1.0 + p
            coeff = p / d
            prod = (d[0:8] * d[8:16]) * (d[16:24] * d[24:32])
            loss = jnp.log(prod)
            t = 2 * kp + i // 4
            if k == 0:
                cid = lax.broadcasted_iota(jnp.int32, (32, ROWS), 0) + (own_base[t] * ROWS + (i % 4) * 32)
                hit = cid == PI[s, 0:1]
                coeff = jnp.where(hit, coeff - 1.0, coeff)
                loss = loss - fold(jnp.where(hit, logits, 0.0))
            C[k, t, (i % 4) * 32:(i % 4) * 32 + 32, cols] = coeff.astype(jnp.bfloat16)
            new = (loss, fold(coeff * ts), fold(coeff))
            tot = new if tot is None else tuple(u + v for u, v in zip(tot, new))
        for j in range(3):
            SUMS[j] += tot[j]

    arrived("KS", K.at[0, SIB])
    pair_terms(0, 0, OWN)

    arrived("QRa", Q.at[LEFT, a_half])
    send("QFR", Q.at[LEFT, a_half], Q.at[OPP, a_half], right)
    arrived("QLb", Q.at[RIGHT, b_half])
    send("QFL", Q.at[RIGHT, b_half], Q.at[OPP, b_half], left)
    arrived("KYa", K.at[0, YP, a_half])

    @pl.when(not_last)
    def _():
        send("FZ", K.at[0, YP, a_half], K.at[1, YP, a_half], z_next, keep=False)

    send("S0a", K.at[0, YP, a_half], K.at[0, YS, a_half], sib)
    arrived("KZb", K.at[1, OWN, b_half])

    @pl.when(not_first)
    def _():
        send("FY", K.at[1, OWN, b_half], K.at[1, YP, b_half], y_peer, keep=False)

    send("S1b", K.at[1, OWN, b_half], K.at[1, SIB, b_half], sib)
    arrived("KYb", K.at[0, YP, b_half])
    send("S0b", K.at[0, YP, b_half], K.at[0, YS, b_half], sib)
    arrived("KZa", K.at[1, OWN, a_half])
    send("S1a", K.at[1, OWN, a_half], K.at[1, SIB, a_half], sib)
    arrived("QRb", Q.at[LEFT, b_half])
    arrived("QLa", Q.at[RIGHT, a_half])
    arrived("PIR", PI.at[LEFT])
    arrived("PIL", PI.at[RIGHT])
    pair_terms(0, 0, LEFT)
    pair_terms(0, 0, RIGHT)
    arrived("S0a", K.at[0, YS, a_half])
    arrived("S0b", K.at[0, YS, b_half])
    for s in (OWN, LEFT, RIGHT):
        pair_terms(0, 1, s)
    arrived("FZ", K.at[1, YP, a_half])
    send("S2a", K.at[1, YP, a_half], K.at[1, YS, a_half], sib)
    arrived("FY", K.at[1, YP, b_half])
    send("S2b", K.at[1, YP, b_half], K.at[1, YS, b_half], sib)
    arrived("S1b", K.at[1, SIB, b_half])
    arrived("S1a", K.at[1, SIB, a_half])
    for s in (OWN, LEFT, RIGHT):
        pair_terms(1, 0, s)
    arrived("PIO", PI.at[OPP])
    arrived("QFR", Q.at[OPP, a_half])
    arrived("QFL", Q.at[OPP, b_half])
    pair_terms(0, 0, OPP)
    pair_terms(0, 1, OPP)

    def key_part(k, slots):
        coeff = jnp.concatenate([C[k, t] for t in slots], axis=0)
        return jnp.dot(coeff, Q[...].reshape(4 * ROWS, E), preferred_element_type=jnp.float32)

    def swap(k):
        rows = pl.ds(ROWS, ROWS)
        SS[k] = key_part(k, (SIB, YS))
        send("G%dy" % k, SS.at[k, rows], RS.at[k, rows], sib)
        rows = pl.ds(0, ROWS)
        send("G%do" % k, SS.at[k, rows], RS.at[k, rows], sib)

    swap(0)
    pair_terms(1, 0, OPP)
    arrived("S2a", K.at[1, YS, a_half])
    arrived("S2b", K.at[1, YS, b_half])
    for s in (OWN, LEFT, RIGHT, OPP):
        pair_terms(1, 1, s)

    def image_part(slots):
        cols = slice(slots[0] * ROWS, (slots[-1] + 1) * ROWS)
        out = None
        for k in range(WINDOW):
            new = lax.dot_general(C[k, :, :, cols].reshape(4 * ROWS, -1), K[k].reshape(4 * ROWS, E), TN,
                                  preferred_element_type=jnp.float32)
            out = new if out is None else out + new
        for i, s in enumerate(slots):
            ACCQ[s] = out[i * ROWS:(i + 1) * ROWS]

    def code(name, terms):
        p = PARTS.index(name)

        def body(j, _):
            cs = pl.ds(pl.multiple_of(j * LANES, LANES), LANES)
            v = None
            for t in terms:
                if isinstance(t, str):
                    q = PARTS.index(t)
                    u = RP[q, :, cs].astype(jnp.int32).astype(jnp.float32) * RPS[q, :, cs]
                else:
                    u = t[0][t[1], cs]
                v = u if v is None else v + u
            m = jnp.max(jnp.abs(v), axis=0, keepdims=True)
            up = 32767.0 / jnp.maximum(m, 1e-30)
            SP[p, :, cs] = jnp.round(v * up).astype(jnp.int32).astype(jnp.int16)
            SPS[p, :, cs] = m * (1.0 / 32767.0)
            return 0
        lax.fori_loop(0, E // LANES, body, 0, unroll=3)

    def send_part(name, peer, to=None, keep=True):
        p = PARTS.index(name)
        q = p if to is None else PARTS.index(to)
        send(name, SP.at[p], RP.at[q], peer, to, keep)
        send(SCALES + p, SPS.at[p], RPS.at[q], peer, SCALES + q, keep)

    def send_two(name, to, other):
        p, q, r = PARTS.index(name), PARTS.index(to), PARTS.index(other)
        for lo in range(0, H, 32):
            rows = pl.ds(lo, 32)
            send(name, SP.at[p, rows], RP.at[q, rows], zy_prev, to, False)
            send(other, SP.at[r, rows], RP.at[r, rows], z_prev, None, False)
        send(SCALES + p, SPS.at[p], RPS.at[q], zy_prev, SCALES + q, False)
        send(SCALES + r, SPS.at[r], RPS.at[r], z_prev, None, False)

    def part(name, terms, peer):
        code(name, terms)
        send_part(name, peer)

    def part_in(name):
        p = PARTS.index(name)
        arrived(name, RP.at[p])
        arrived(SCALES + p, RPS.at[p])

    swap(1)

    row = lax.broadcasted_iota(jnp.int32, (8, LANES), 0)
    mine = jnp.zeros((8, LANES), jnp.float32)
    for j in range(3):
        mine = jnp.where(row == j, jnp.sum(SUMS[j], axis=0, keepdims=True), mine)
    ST[0] = mine
    for i, peer in enumerate(stage1):
        send("T0%d" % i, ST.at[0], RT.at[0, i], peer)

    def stage_sum(st, peers):
        tot = ST[st]
        for i in range(len(peers)):
            arrived("T%d%d" % (st, i), RT.at[st, i])
            tot = tot + RT[st, i]
        return tot

    image_part((OPP,))
    part("XOa", [(ACCQ.at[OPP], a_half)], right)
    part("XOb", [(ACCQ.at[OPP], b_half)], left)
    ACCK[1] = key_part(1, (OWN, YP))
    arrived("G1y", RS.at[1, pl.ds(ROWS, ROWS)])
    own_a, own_b, y_a, y_b = pl.ds(0, H), pl.ds(H, H), pl.ds(2 * H, H), pl.ds(3 * H, H)
    code("Y1a", [(ACCK.at[1], y_a), (RS.at[1], y_a)])

    @pl.when(last)
    def _():
        send_part("Y1a", z_prev, "Z1a", keep=False)

    @pl.when(inner)
    def _():
        send_part("Y1a", y_peer, keep=False)

    arrived("G1o", RS.at[1, pl.ds(0, ROWS)])
    zob = [(ACCK.at[1], own_b), (RS.at[1], own_b)]
    zoa = [(ACCK.at[1], own_a), (RS.at[1], own_a)]

    @pl.when(first)
    def _():
        code("Zob", zob)
        send_two("Y1a", "DA", "Zob")

    code("Z1b", [(ACCK.at[1], y_b), (RS.at[1], y_b)])

    @pl.when(first)
    def _():
        code("Zoa", zoa)
        send_two("Z1b", "DB", "Zoa")

    @pl.when(not_first)
    def _():
        send_part("Z1b", z_prev, keep=False)

    image_part((LEFT, RIGHT))
    part("XRb", [(ACCQ.at[RIGHT], b_half)], right)
    part("XLa", [(ACCQ.at[LEFT], a_half)], left)

    @pl.when(not_first)
    def _():
        code("Zob", zob)
        send_part("Zob", z_prev, keep=False)

    ACCK[0] = key_part(0, (OWN, YP))
    arrived("G0y", RS.at[0, pl.ds(ROWS, ROWS)])
    arrived("G0o", RS.at[0, pl.ds(0, ROWS)])
    y0a = [(ACCK.at[0], y_a), (RS.at[0], y_a)]

    @pl.when(not_before_last)
    def _():
        code("Y0a", y0a)
        send_part("Y0a", y_peer, keep=False)

    ST[1] = stage_sum(0, stage1)
    for i, peer in enumerate(stage2):
        send("T1%d" % i, ST.at[1], RT.at[1, i], peer)

    part_in("XOa")
    part("XRa", [(ACCQ.at[RIGHT], a_half), "XOa"], right)
    part_in("XOb")
    part("XLb", [(ACCQ.at[LEFT], b_half), "XOb"], left)
    @pl.when(last)
    def _():
        code("Zoa", zoa)
        send_part("Zoa", z_prev, keep=False)

    @pl.when(inner)
    def _():
        part_in("Y1a")
        code("Zoa", zoa + ["Y1a"])
        send_part("Zoa", z_prev, keep=False)

    y0b = [(ACCK.at[0], y_b), (RS.at[0], y_b)]

    @pl.when(before_last)
    def _():
        part_in("Z1a")
        code("Y0a", y0a + ["Z1a"])
        send_part("Y0a", y_peer, keep=False)

    @pl.when(last)
    def _():
        code("Y0b", y0b)

    @pl.when(not_last)
    def _():
        part_in("Z1b")
        code("Y0b", y0b + ["Z1b"])

    send_part("Y0b", y_peer)
    image_part((OWN,))

    ST[2] = stage_sum(1, stage2)
    for i, peer in enumerate(stage3):
        send("T2%d" % i, ST.at[2], RT.at[2, i], peer)

    def finish(half, src, which, own, parts, out):
        def body(i, _):
            local = pl.ds(pl.multiple_of(i * 16, 16), 16)
            rows = pl.ds(pl.multiple_of(half * H + i * 16, 16), 16)
            inv = INV[which, rows, 0:1]
            unit = src[rows, :].astype(jnp.float32) * inv
            grad = None
            for o in own:
                grad = o[rows, :] if grad is None else grad + o[rows, :]
            for name in parts:
                q = PARTS.index(name)
                grad = grad + RP[q, local, :].astype(jnp.int32).astype(jnp.float32) * RPS[q]
            along = jnp.sum(unit * grad, axis=1, keepdims=True)
            out[rows, :] = inv * (grad - unit * along)
            return 0
        lax.fori_loop(0, H // 16, body, 0, unroll=2)

    key_own = [ACCK.at[0], RS.at[0]]
    part_in("XRb")
    part_in("XLb")
    finish(1, IM, 0, [ACCQ.at[OWN]], ["XRb", "XLb"], GI)
    part_in("XRa")
    part_in("XLa")
    finish(0, IM, 0, [ACCQ.at[OWN]], ["XRa", "XLa"], GI)
    part_in("Zoa")
    part_in("Y0a")

    def finish_caption(half, names, extra):
        @pl.when(last)
        def _():
            part_in(extra)
            finish(half, CAP, 1, key_own, names + [extra], GC)

        @pl.when(not_last)
        def _():
            finish(half, CAP, 1, key_own, names, GC)


    finish_caption(0, ["Zoa", "Y0a"], "DA")
    part_in("Zob")
    part_in("Y0b")
    finish_caption(1, ["Zob", "Y0b"], "DB")

    tot = stage_sum(2, stage3)
    count = 1.0 / (n_blk * WINDOW * 2048.0 * 2048.0)
    for j, ref in ((0, loss_ref), (1, gs_ref), (2, gb_ref)):
        ref[0] = jnp.sum(tot[j:j + 1, :]) * count
    for c in sent:
        c.wait_send()
    copy("FZ", K.at[0, OWN, a_half], K.at[1, YP, a_half], sib).wait_send()
    copy("KZb", K.at[0, OWN, b_half], K.at[1, OWN, b_half], sib).wait_send()
    copy("KZa", K.at[0, OWN, a_half], K.at[1, OWN, a_half], sib).wait_send()
    for name in ("Y1a", "Z1b", "Y0a", "Zob", "Zoa"):
        p = PARTS.index(name)
        copy(name, SP.at[p], RP.at[p], sib).wait_send()
        copy(SCALES + p, SPS.at[p], RPS.at[p], sib).wait_send()

    @pl.when(last)
    def _():
        copy("EB", K.at[0, OWN, b_half], K.at[1, YP, b_half], zy_next, "FY").wait_send()

    @pl.when(not_first)
    def _():
        copy("FY", K.at[1, OWN, b_half], K.at[1, YP, b_half], y_peer).wait_send()


def on_device(n_blk, images, captions, pair_index, logit_scale, logit_bias):
    smem = pl.BlockSpec(memory_space=pltpu.SMEM)
    hbm = pl.BlockSpec(memory_space=pltpu.HBM)
    vmem = pl.BlockSpec(memory_space=pltpu.VMEM)
    f32, bf16, i16 = jnp.float32, jnp.bfloat16, jnp.int16
    one = jax.ShapeDtypeStruct((1,), f32)
    grad = jax.ShapeDtypeStruct((ROWS, E), f32)
    unit = (ROWS, E)
    n = len(PARTS)
    loss, grad_images, grad_captions, grad_scale, grad_bias = pl.pallas_call(
        functools.partial(kernel, n_blk),
        out_shape=(one, grad, grad, one, one),
        in_specs=[hbm, hbm, hbm, smem, smem],
        out_specs=(smem, vmem, vmem, smem, smem),
        scratch_shapes=[
            pltpu.VMEM(unit, bf16),
            pltpu.VMEM(unit, bf16),
            pltpu.VMEM((1, LANES), jnp.int32),
            pltpu.VMEM((4,) + unit, bf16),
            pltpu.VMEM((4, 8, LANES), jnp.int32),
            pltpu.VMEM((2, 4) + unit, bf16),
            pltpu.VMEM((2, 4, ROWS, 4 * ROWS), bf16),
            pltpu.VMEM((2, ROWS, LANES), f32),
            pltpu.VMEM((4,) + unit, f32),
            pltpu.VMEM((2, 2 * ROWS, E), f32),
            pltpu.VMEM((2, 2 * ROWS, E), f32),
            pltpu.VMEM((2, 2 * ROWS, E), f32),
            pltpu.VMEM((n, H, E), i16),
            pltpu.VMEM((n, 1, E), f32),
            pltpu.VMEM((n, H, E), i16),
            pltpu.VMEM((n, 1, E), f32),
            pltpu.VMEM((3, 8, LANES), f32),
            pltpu.VMEM((3, 7, 8, LANES), f32),
            pltpu.VMEM((3, 8, LANES), f32),
            pltpu.SemaphoreType.DMA((3,)),
            pltpu.SemaphoreType.DMA((N_MSG,)),
            pltpu.SemaphoreType.DMA((N_MSG,)),
        ],
        compiler_params=pltpu.CompilerParams(
            collective_id=0, has_side_effects=True, vmem_limit_bytes=60 * 2**20),
    )(images, captions, pair_index, logit_scale, logit_bias)
    temper = jnp.exp(logit_scale[0])
    return loss, temper * grad_images, temper * grad_captions, grad_scale, grad_bias


def solution(mesh):
    placed = (P(("blk", "gather"), None), P(("blk", "gather"), None), P("blk", "gather"), P(), P())
    return jax.shard_map(
        functools.partial(on_device, mesh.shape["blk"]),
        mesh=mesh,
        in_specs=placed,
        out_specs=(P(), P(("blk", "gather"), None), P(("blk", "gather"), None), P(), P()),
        check_vma=False,
    )
```
